512 devices in a mesh: gx: 8 (over x, z_hi), gy: 8 (over y, core), gz: 8 (over z_lo).
Axes of the slice: x: 4, y: 4, z: 16 (z_hi: 2, z_lo: 8; z = z_hi * 8 + z_lo), core: 2. Of those that a mesh axis runs over, the one named last changes fastest.
Arguments:
- positions: float32 [8, 8, 16, 3, 128], P('gx', 'gy', 'gz'), may hold values from 0 to 16, as said below
- block_fill: int32 [8, 8, 16], P('gx', 'gy', 'gz'), may hold values from 16 to 128, as said below
- noise: float32 [8, 8, 16, 8, 384], P('gx', 'gy', 'gz'), may hold values from -6 to 6
- pair_list: int32 [8, 8, 8, 3, 54], P('gx', 'gy', 'gz'), may hold values from 0 to 26, as said below
- pair_count: int32 [8, 8, 8], P('gx', 'gy', 'gz'), may hold values from 2 to 54, as said below
Outputs:
- displacement: float32 [8, 8, 16, 8, 384], P('gx', 'gy', 'gz')
The draws below stay inside these ranges and needn't reach their ends.
Inputs may be any that keep to these rules, and one draw needn't show every extreme that they name: `positions`: each bead of cell (x, y, z) lies in the unit cube with corner (x, y, z). `block_fill`: beads of a block occupy its first slots. `pair_list`: in each device's list, the first pair_count slots hold field 0, a block index below 2; field 1, a neighbour code 9 (dx + 1) + 3 (dy + 1) + (dz + 1) with dx, dy, dz in -1..1 whose cell lies inside the grid; field 2, the owner flag. The relation is symmetric: a pair is listed on the first block's device exactly when the reverse pair is listed on the second block's device, and exactly one of the two carries owner flag 1; every block lists itself with code 13 and flag 1. Later slots hold 0, 13, 0. `pair_count`: counts the listed pairs of the device, each block's own pair included; some device lists every neighbour inside the grid of each of its blocks.
All inputs are finite; a program needn't handle non-finite values.
Results may differ from the reference program's by a relative error of at most 0.0025.
Values may be sent and summed in bfloat16 or wider, within the bound.
A program may use at most 64 MiB of HBM per device.

```python
import jax
import jax.numpy as jnp
from jax import lax

BEAD = 128
BLK_Z = 2
SAMPLES = 8
ITERS = 3
ROOT_ITERS = 12
NX = 8
NY = 8
NZ = 16
PAIR_CAP = 54
N_GX = 8
N_GY = 8
N_GZ = 8


def draw_positions(key, part):
    jitter = jax.random.uniform(key, (NX, NY, NZ, 3, BEAD), jnp.float32)
    corner = jnp.stack([lax.broadcasted_iota(jnp.float32, (NX, NY, NZ), axis_number) for axis_number in range(3)], axis=3)
    return corner[..., None] + jitter


def draw_block_fill(key, part):
    first_index = lax.broadcasted_iota(jnp.int32, (NX, NY, NZ), 0)
    lower_bound = BEAD // 8 + 5 * BEAD // 8 * first_index // max(NX - 1, 1)
    spread_draw = jax.random.randint(key, (NX, NY, NZ), 0, BEAD // 4 + 1)
    return (lower_bound + spread_draw).astype(jnp.int32)


def pair_tables(key):
    level_key, test_key, owner_key = jax.random.split(key, 3)
    devices_z = NZ // BLK_Z
    level_draw = jax.random.randint(level_key, (NX, NY, devices_z), 0, 101)
    device_level = level_draw * level_draw // 100
    device_level = device_level.at[NX // 2, NY // 2, devices_z // 2].set(100)
    cell_level = jnp.repeat(device_level, BLK_Z, axis=2)
    pair_tests = jax.random.randint(test_key, (27, NX, NY, NZ), 0, 100)
    coin_flips = jax.random.randint(owner_key, (27, NX, NY, NZ), 0, 2)
    coord_x = lax.broadcasted_iota(jnp.int32, (NX, NY, NZ), 0)
    coord_y = lax.broadcasted_iota(jnp.int32, (NX, NY, NZ), 1)
    coord_z = lax.broadcasted_iota(jnp.int32, (NX, NY, NZ), 2)
    live_list = []
    owner_list = []
    for neighbour_code in range(27):
        shift_x = neighbour_code // 9 - 1
        shift_y = neighbour_code // 3 % 3 - 1
        shift_z = neighbour_code % 3 - 1
        inside = (coord_x + shift_x >= 0) & (coord_x + shift_x < NX) & (coord_y + shift_y >= 0) & (coord_y + shift_y < NY) & (coord_z + shift_z >= 0) & (coord_z + shift_z < NZ)
        partner_level = jnp.roll(cell_level, (-shift_x, -shift_y, -shift_z), axis=(0, 1, 2))
        pair_level = jnp.maximum(cell_level, partner_level)
        if neighbour_code == 13:
            live_now = jnp.ones((NX, NY, NZ), jnp.int32)
            owner_now = jnp.ones((NX, NY, NZ), jnp.int32)
        elif neighbour_code > 13:
            live_now = (inside & (pair_tests[neighbour_code] < pair_level)).astype(jnp.int32)
            owner_now = coin_flips[neighbour_code]
        else:
            mirror_code = 26 - neighbour_code
            mirror_test = jnp.roll(pair_tests[mirror_code], (-shift_x, -shift_y, -shift_z), axis=(0, 1, 2))
            live_now = (inside & (mirror_test < pair_level)).astype(jnp.int32)
            owner_now = 1 - jnp.roll(coin_flips[mirror_code], (-shift_x, -shift_y, -shift_z), axis=(0, 1, 2))
        live_list.append(live_now)
        owner_list.append(owner_now)
    flat_live = jnp.stack(live_list, axis=3).reshape(NX, NY, devices_z, PAIR_CAP)
    flat_owner = jnp.stack(owner_list, axis=3).reshape(NX, NY, devices_z, PAIR_CAP)
    slot_ids = lax.broadcasted_iota(jnp.int32, flat_live.shape, 3)
    ranking = jnp.where(flat_live == 1, slot_ids, slot_ids + PAIR_CAP)
    ranked_order = jnp.argsort(ranking, axis=3, stable=True).astype(jnp.int32)
    sorted_live = jnp.take_along_axis(flat_live, ranked_order, axis=3)
    block_index = jnp.where(sorted_live == 1, ranked_order // 27, 0)
    code_field = jnp.where(sorted_live == 1, ranked_order % 27, 13)
    owner_field = jnp.where(sorted_live == 1, jnp.take_along_axis(flat_owner, ranked_order, axis=3), 0)
    table = jnp.stack([block_index, code_field, owner_field], axis=3).astype(jnp.int32)
    totals = jnp.sum(flat_live, axis=3).astype(jnp.int32)
    return (table, totals)


def draw_pair_list(key, part):
    table, totals = pair_tables(jax.random.fold_in(key, 11))
    return table


def draw_pair_count(key, part):
    table, totals = pair_tables(jax.random.fold_in(key, 11))
    return totals


def levels(key, extent, shards, low, top_value):
    level, own = 1.0, jax.random.fold_in(key, 6)
    for position, parts in shards:
        steps = jnp.exp(jax.random.uniform(jax.random.fold_in(own, position), (parts,), jnp.float32, low / len(shards), top_value / len(shards)))
        level = level * jnp.repeat(steps, extent[position] // parts).reshape([-1 if axis == position else 1 for axis in range(len(extent))])
    return level


def normal_values(stream_key, shape, spread, reach, shards=(), held_as=jnp.bfloat16):
    drawn = spread * jax.random.normal(stream_key, shape, jnp.float32)
    if shards:
        drawn = drawn * levels(stream_key, shape, shards, -0.22, 0.18)
    return jnp.clip(drawn, -reach, reach).astype(held_as)


def setup_inputs(seed: int = 0) -> dict:
    key_of = jax.random.split(jax.random.key(seed), 6)
    positions = draw_positions(jax.random.fold_in(key_of[5], 71), 0)
    block_fill = draw_block_fill(jax.random.fold_in(key_of[5], 71), 0)
    noise = normal_values(key_of[2], (NX, NY, NZ, SAMPLES, 3 * BEAD), 1.0, 6.0, ((0, 8), (1, 8), (2, 8)), jnp.float32)
    pair_list = draw_pair_list(jax.random.fold_in(key_of[5], 71), 0)
    pair_count = draw_pair_count(jax.random.fold_in(key_of[5], 71), 0)
    return {"positions": positions, "block_fill": block_fill, "noise": noise, "pair_list": pair_list, "pair_count": pair_count}


radius = 0.08
floor_sq = 0.0001
epsilon = 1e-06
group_pairs = 32

def mobility_tiles(first_pos, second_pos):
    offset = second_pos[:, :, None, :] - first_pos[:, :, :, None]
    dist_sq = offset[:, 0] * offset[:, 0] + offset[:, 1] * offset[:, 1] + offset[:, 2] * offset[:, 2]
    inverse_sq = 1.0 / jnp.maximum(dist_sq, floor_sq)
    distance = jnp.sqrt(dist_sq)
    reach_ratio = radius * jnp.sqrt(inverse_sq)
    far_iso = 0.75 * reach_ratio * (1.0 + 2.0 / 3.0 * radius * radius * inverse_sq)
    far_dyad = 0.75 * reach_ratio * (1.0 - 2.0 * radius * radius * inverse_sq)
    near_iso = 1.0 - 9.0 / 32.0 * distance / radius
    near_dyad = 3.0 / 32.0 * distance / radius
    apart = dist_sq >= 4.0 * radius * radius
    isotropic = jnp.where(apart, far_iso, near_iso)
    dyadic = jnp.where(apart, far_dyad, near_dyad) * inverse_sq
    identity_three = jnp.eye(3, dtype=jnp.float32)
    offset_t = jnp.transpose(offset, (0, 2, 1, 3))
    product = offset[:, :, :, None, :] * offset_t[:, None, :, :, :]
    mobility = identity_three[None, :, None, :, None] * isotropic[:, None, :, None, :] + dyadic[:, None, :, None, :] * product
    group_size = first_pos.shape[0]
    bead_count = first_pos.shape[2]
    return mobility.reshape(group_size, 3 * bead_count, 3 * bead_count).astype(jnp.bfloat16)

def inverse_three(matrix):
    cofactor = [[matrix[(line_index + 1) % 3][(place_index + 1) % 3] * matrix[(line_index + 2) % 3][(place_index + 2) % 3] - matrix[(line_index + 1) % 3][(place_index + 2) % 3] * matrix[(line_index + 2) % 3][(place_index + 1) % 3] for place_index in range(3)] for line_index in range(3)]
    determinant = matrix[0][0] * cofactor[0][0] + matrix[0][1] * cofactor[0][1] + matrix[0][2] * cofactor[0][2]
    return [[cofactor[place_index][line_index] / determinant for place_index in range(3)] for line_index in range(3)]

def root_first_column(diagonal, coupling):
    zero_entry = jnp.zeros_like(diagonal[0])
    one_entry = jnp.ones_like(diagonal[0])
    trace_scale = (diagonal[0] + diagonal[1] + diagonal[2]) / 3.0
    tridiagonal = [[diagonal[0], coupling[0], zero_entry], [coupling[0], diagonal[1], coupling[1]], [zero_entry, coupling[1], diagonal[2]]]
    root_guess = [[matrix_entry / trace_scale for matrix_entry in matrix_line] for matrix_line in tridiagonal]
    partner = [[one_entry if line_index == place_index else zero_entry for place_index in range(3)] for line_index in range(3)]
    for repeat_index in range(ROOT_ITERS):
        inverse_partner = inverse_three(partner)
        inverse_guess = inverse_three(root_guess)
        root_guess, partner = ([[0.5 * (root_guess[line_index][place_index] + inverse_partner[line_index][place_index]) for place_index in range(3)] for line_index in range(3)], [[0.5 * (partner[line_index][place_index] + inverse_guess[line_index][place_index]) for place_index in range(3)] for line_index in range(3)])
    root_scale = jnp.sqrt(trace_scale)
    return [root_scale * root_guess[line_index][0] for line_index in range(3)]

def local_dot(left, right):
    return lax.optimization_barrier(jnp.sum(left * right, axis=(0, 1, 2, 4)))

def reference(positions, block_fill, noise, pair_list, pair_count):
    row_width = 3 * BEAD
    cell_total = NX * NY * NZ
    bead_slots = lax.broadcasted_iota(jnp.int32, (NX, NY, NZ, BEAD), 3)
    live_mask = jnp.tile((bead_slots < block_fill[..., None]).astype(jnp.float32), (1, 1, 1, 3))[:, :, :, None, :]
    flat_pos = positions.reshape(cell_total, 3, BEAD)
    padded_pos = jnp.pad(positions, ((1, 1), (1, 1), (1, 1), (0, 0), (0, 0))).reshape(-1, 3, BEAD)
    block_ids = pair_list[:, :, :, 0, :]
    neighbour_codes = pair_list[:, :, :, 1, :]
    list_shape = block_ids.shape
    device_x = lax.broadcasted_iota(jnp.int32, list_shape, 0)
    device_y = lax.broadcasted_iota(jnp.int32, list_shape, 1)
    device_z = lax.broadcasted_iota(jnp.int32, list_shape, 2)
    slot_ids = lax.broadcasted_iota(jnp.int32, list_shape, 3)
    valid_mask = (slot_ids < pair_count[..., None]).astype(jnp.float32)
    cell_z = device_z * BLK_Z + block_ids
    home_cells = (device_x * NY + device_y) * NZ + cell_z
    away_cells = ((device_x + neighbour_codes // 9) * (NY + 2) + device_y + neighbour_codes // 3 % 3) * (NZ + 2) + cell_z + neighbour_codes % 3
    entry_total = N_GX * N_GY * N_GZ * PAIR_CAP
    group_count = (entry_total + group_pairs - 1) // group_pairs
    padding_size = group_count * group_pairs - entry_total

    def arrange(values):
        return jnp.pad(values.reshape(-1), (0, padding_size)).reshape(group_count, group_pairs)
    home_groups = arrange(home_cells.astype(jnp.int32))
    away_groups = arrange(away_cells.astype(jnp.int32))
    weight_groups = arrange(valid_mask)

    def apply_mobility(vector_bf):
        padded = jnp.pad(vector_bf, ((1, 1), (1, 1), (1, 1), (0, 0), (0, 0))).reshape(-1, SAMPLES, row_width)

        def accumulate(running, group_data):
            home_pick, away_pick, weight_pick = group_data
            mobility = mobility_tiles(flat_pos[home_pick], padded_pos[away_pick])
            contribution = jnp.einsum('gsk,gmk->gsm', padded[away_pick].astype(jnp.float32), mobility.astype(jnp.float32), precision=lax.Precision.HIGHEST)
            return (running.at[home_pick].add(contribution * weight_pick[:, None, None]), None)
        running, unused = lax.scan(accumulate, jnp.zeros((cell_total, SAMPLES, row_width), jnp.float32), (home_groups, away_groups, weight_groups))
        return running.reshape(NX, NY, NZ, SAMPLES, row_width) * live_mask
    start_vec = noise * live_mask
    start_norm = jnp.sqrt(local_dot(start_vec, start_vec) + epsilon)
    current = start_vec / start_norm[:, None]
    previous = jnp.zeros_like(current)
    beta_prev = jnp.zeros((SAMPLES,), jnp.float32)
    basis = []
    diagonal = []
    coupling = []
    for repeat_index in range(ITERS):
        basis.append(current)
        image_vec = apply_mobility(current.astype(jnp.bfloat16))
        alpha_now = local_dot(current, image_vec)
        diagonal.append(alpha_now)
        if repeat_index + 1 < ITERS:
            residual = image_vec - alpha_now[:, None] * current - beta_prev[:, None] * previous
            beta_now = jnp.sqrt(local_dot(residual, residual) + epsilon)
            coupling.append(beta_now)
            previous = current
            current = residual / beta_now[:, None]
            beta_prev = beta_now
    weights = root_first_column(diagonal, coupling)
    result = (start_norm * weights[0])[:, None] * basis[0]
    for repeat_index in range(1, ITERS):
        result = result + (start_norm * weights[repeat_index])[:, None] * basis[repeat_index]
    return result
```

```python
import jax
import jax.numpy as jnp
from jax import lax
from jax.experimental import pallas as pl
from jax.experimental.pallas import tpu as pltpu
from jax.sharding import PartitionSpec as P

ROOT_ITERS = 12
RADIUS = 0.08
EPSILON = 1e-6
MESH = pl.DeviceIdType.MESH
BEAD = 128
SAMPLES = 8
CELL = 3 * SAMPLES
LEFT, MID, RIGHT = (0, 32), (32, 48), (80, 32)
PAIRS = ((0, 0), (0, 1), (1, 1), (0, 2), (1, 2), (1, 3))
f32, bf16 = jnp.float32, jnp.bfloat16


def tile_factors(d0, d1, d2):
    dist = d0 * d0 + d1 * d1 + d2 * d2
    root = lax.rsqrt(jnp.maximum(dist, 1e-30))
    capped = jnp.minimum(root, 100.0)
    inv = capped * capped
    length = dist * root
    far_iso = capped * (0.75 * RADIUS + (0.5 * RADIUS**3) * inv)
    far_dyad = capped * (0.75 * RADIUS - (1.5 * RADIUS**3) * inv)
    near_iso = 1.0 - (9.0 / 32.0 / RADIUS) * length
    near_dyad = (3.0 / 32.0 / RADIUS) * length
    apart = dist >= 4.0 * RADIUS * RADIUS
    return jnp.where(apart, far_iso, near_iso), jnp.where(apart, far_dyad, near_dyad) * inv


def inverse_three(m):
    def cof(i, j):
        a, b, c, d = (i + 1) % 3, (i + 2) % 3, (j + 1) % 3, (j + 2) % 3
        return m[a][c] * m[b][d] - m[a][d] * m[b][c]

    co = [[cof(i, j) for j in range(3)] for i in range(3)]
    scale = 1.0 / (m[0][0] * co[0][0] + m[0][1] * co[0][1] + m[0][2] * co[0][2])
    return [[co[j][i] * scale for j in range(3)] for i in range(3)]


def combination(moments):
    def inner(left, right):
        total = 0.0
        for i, a in enumerate(left):
            for j, b in enumerate(right):
                total = total + a * b * moments[i + j]
        return total

    def apply(v):
        return [v[0]] + [v[i] + v[i - 1] for i in range(1, len(v))] + [v[-1]]

    norm = jnp.sqrt(moments[0] + EPSILON)
    v1 = [1.0 / norm]
    w1 = apply(v1)
    a1 = inner(v1, w1)
    r1 = [w1[0] - a1 * v1[0], w1[1]]
    b1 = jnp.sqrt(inner(r1, r1) + EPSILON)
    v2 = [r / b1 for r in r1]
    w2 = apply(v2)
    a2 = inner(v2, w2)
    r2 = [w2[0] - a2 * v2[0] - b1 * v1[0], w2[1] - a2 * v2[1], w2[2]]
    b2 = jnp.sqrt(inner(r2, r2) + EPSILON)
    v3 = [r / b2 for r in r2]
    a3 = inner(v3, apply(v3))
    scale = (a1 + a2 + a3) / 3.0
    zero, one = jnp.zeros_like(a1), jnp.ones_like(a1)
    y = [[e / scale for e in row] for row in ((a1, b1, zero), (b1, a2, b2), (zero, b2, a3))]
    z = [[one if i == j else zero for j in range(3)] for i in range(3)]

    def step(_, state):
        y, z = state
        iz, iy = inverse_three(z), inverse_three(y)
        return (
            [[0.5 * (y[i][j] + iz[i][j]) for j in range(3)] for i in range(3)],
            [[0.5 * (z[i][j] + iy[i][j]) for j in range(3)] for i in range(3)],
        )

    y, z = lax.fori_loop(0, ROOT_ITERS, step, (y, z))
    root = [jnp.sqrt(scale) * y[i][0] for i in range(3)]
    return [
        norm * (root[0] * v1[0] + root[1] * v2[0] + root[2] * v3[0]),
        norm * (root[1] * v2[1] + root[2] * v3[1]),
        norm * (root[2] * v3[2]),
    ]


def kernel(
    fill_ref, count_ref, list_ref, pos_ref, noise_ref, out_ref,
    meta_src, start_src, pos_halo, start_own, halo, own, back, tiles, columns, weights,
    sums_z, sums_xy, row_buf,
    move_send, move_recv, back_send, back_recv, pos_send, pos_recv, u_send, u_recv,
    z_send, z_recv, xy_send, xy_recv,
):
    ix, iy, iz = lax.axis_index("gx"), lax.axis_index("gy"), lax.axis_index("gz")
    nx = lax.axis_size("gx") // 2
    ny = lax.axis_size("gy")
    half = lax.axis_size("gz")
    nz = 2 * half
    my_x, my_z = lax.div(ix, 2), lax.rem(ix, 2) * half + iz

    def device(x, y, z):
        return (2 * x + lax.div(z, half), y, lax.rem(z, half))

    def shifted(dx, dy, dz):
        return device(
            lax.rem(my_x + dx + nx, nx), lax.rem(iy + dy + ny, ny), lax.rem(my_z + dz + nz, nz)
        )

    barrier = pltpu.get_barrier_semaphore()

    def greet(dx, dy, dz):
        pl.semaphore_signal(barrier, inc=1, device_id=shifted(dx, dy, dz), device_id_type=MESH)

    @pl.loop(1, nz)
    def _(k):
        greet(0, 0, k)

    @pl.loop(1, nx * ny)
    def _(k):
        greet(lax.div(k, ny), lax.rem(k, ny), 0)

    @pl.loop(0, 16)
    def _(k):
        q = lax.rem(k, 8)
        q = q + lax.div(q + 4, 8)
        greet(lax.div(q, 3) - 1, lax.rem(q, 3) - 1, 2 * lax.div(k, 8) - 1)

    lanes = lax.broadcasted_iota(jnp.int32, (1, BEAD), 1)
    slots = list_ref.shape[1]
    codes = lax.broadcasted_iota(jnp.int32, (BEAD, slots), 0)
    live = lax.broadcasted_iota(jnp.int32, (1, slots), 1) < count_ref[0]
    chosen = jnp.where(codes == list_ref[1:2, :], 1.0, 0.0).astype(bf16)
    masks = []
    for b in range(2):
        mask = jnp.where(lanes < fill_ref[b], 1.0, 0.0)
        masks.append(mask)
        here = jnp.where(live & (list_ref[0:1, :] == b), 1.0, 0.0)
        here = jnp.broadcast_to(here, (SAMPLES, slots)).astype(bf16)
        tally = lax.dot_general(
            here, chosen, (((1,), (1,)), ((), ())), preferred_element_type=f32
        )
        meta_src[b, 0:3, :] = pos_ref[b]
        meta_src[b, 3:4, :] = mask
        meta_src[b, 4:5, :] = tally[0:1]
        meta_src[b, 5:8, :] = jnp.zeros((3, BEAD), f32)
        for c in range(3):
            start_src[b, c * 8 : c * 8 + 8, :] = noise_ref[b, :, c * BEAD : (c + 1) * BEAD] * mask

    pl.semaphore_wait(barrier, (nz - 1) + (nx * ny - 1) + 16)

    def move(src, dst, send, recv, target):
        tx, ty, tz = target
        same = (tx == ix) & (tz == iz)

        @pl.when(same)
        def _():
            pltpu.make_async_copy(src, dst, recv).start()

        @pl.when(jnp.logical_not(same))
        def _():
            pltpu.make_async_remote_copy(
                src, dst, send, recv, device_id=target, device_id_type=MESH
            ).start()

    def moved(src, send, target):
        tx, ty, tz = target
        same = (tx == ix) & (tz == iz)

        @pl.when(jnp.logical_not(same))
        def _():
            pltpu.make_async_remote_copy(
                src, src, send, send, device_id=target, device_id_type=MESH
            ).wait_send()

    def landed(dst, recv):
        pltpu.make_async_copy(dst, dst, recv).wait()

    side = lax.rem(ix, 2)
    for b in range(2):
        target = device(my_x, iy, 2 * iz + b)
        move(meta_src.at[b], pos_halo.at[4, 1 + side], move_send.at[0, b], move_recv.at[0, side], target)
    for b in range(2):
        target = device(my_x, iy, 2 * iz + b)
        move(start_src.at[b], start_own.at[side], move_send.at[1, b], move_recv.at[1, side], target)
    for h in range(2):
        landed(pos_halo.at[4, 1 + h], move_recv.at[0, h])

    def exchange(src_of, dst_of, send, recv):
        def copy(dc, part, dx):
            dy, dz = 1 - lax.rem(dc, 3), 1 - lax.div(dc, 3)
            return pltpu.make_async_remote_copy(
                src_of(part), dst_of(dc, part), send.at[dc, part], recv.at[dc, part],
                device_id=shifted(dx, dy, dz), device_id_type=MESH,
            )

        return copy

    def start_column(copy, dc, middle):
        copy(dc, 0, 1).start()
        copy(dc, 2, -1).start()
        if middle:
            copy(dc, 1, 0).start()

    def sent_column(copy, dc, middle):
        copy(dc, 0, 1).wait_send()
        copy(dc, 2, -1).wait_send()
        if middle:
            copy(dc, 1, 0).wait_send()

    def arrived_column(copy, dc, middle):
        copy(dc, 0, 1).wait_recv()
        copy(dc, 2, -1).wait_recv()
        if middle:
            copy(dc, 1, 0).wait_recv()

    def column(t):
        return lax.rem(t + 4, 9)

    def exchange_start(copy, count):
        start_column(copy, 4, False)

        @pl.loop(1, count)
        def _(t):
            start_column(copy, column(t), True)

    def exchange_sent(copy, count):
        sent_column(copy, 4, False)

        @pl.loop(1, count)
        def _(t):
            sent_column(copy, column(t), True)

    pos_src = {0: (2, 1), 1: (1, 2), 2: (1, 1)}
    pos_dst = {0: (0, 1), 1: (1, 2), 2: (3, 1)}
    pos_copy = exchange(
        lambda part: pos_halo.at[4, pl.ds(*pos_src[part])],
        lambda dc, part: pos_halo.at[dc, pl.ds(*pos_dst[part])],
        pos_send, pos_recv,
    )
    exchange_start(pos_copy, 9)

    own_mask = []
    for h in range(2):
        own_mask.append(pos_halo[4, 1 + h, 3:4, :])
        table = jnp.transpose(pos_halo[4, 1 + h], (1, 0))
        weights[h] = jnp.broadcast_to(table[:, 4:5], (BEAD, BEAD))

    u_src = {0: (48, 32), 1: (32, 48), 2: (32, 32)}
    u_dst = {0: LEFT, 1: MID, 2: RIGHT}

    def u_copy(n):
        return exchange(
            lambda part: halo.at[n, 4, pl.ds(*u_src[part])],
            lambda dc, part: halo.at[n, dc, pl.ds(*u_dst[part])],
            u_send.at[n], u_recv.at[n],
        )

    copies = [u_copy(n) for n in range(3)]
    for h in range(2):
        landed(start_own.at[h], move_recv.at[1, h])
    start = jnp.concatenate([start_own[0], start_own[1]], axis=0)
    own[0] = start
    halo[0, 4, MID[0] : MID[0] + MID[1], :] = start.astype(bf16)
    exchange_start(copies[0], 9)

    def build(dc):
        for xs in range(4):
            columns[xs] = jnp.transpose(pos_halo[dc, xs], (1, 0))
        mine = [[pos_halo[4, 1 + a, c : c + 1, :] for c in range(3)] for a in range(2)]

        @pl.loop(0, BEAD // 16)
        def _(r):
            row = pl.multiple_of(r * 16, 16)
            away = []
            for xs in range(4):
                block = columns[xs, pl.ds(row, 16), :]
                away.append(
                    [jnp.broadcast_to(block[:, c : c + 1], (16, BEAD)) for c in range(3)]
                )
            for q, (a, xs) in enumerate(PAIRS):
                d = [away[xs][c] - mine[a][c] for c in range(3)]
                iso, dyad = tile_factors(*d)
                scaled = [dyad * d[c] for c in range(3)]
                for c in range(3):
                    for e in range(c, 3):
                        entry = scaled[c] * d[e]
                        entry = (entry + iso if c == e else entry).astype(bf16)
                        for e2, c2 in {(e, c), (c, e)}:
                            tiles[
                                dc * 6 + q, pl.ds(e2 * BEAD + row, 16), c2 * BEAD : (c2 + 1) * BEAD
                            ] = entry

    arrived_column(pos_copy, 4, False)
    build(4)

    @pl.loop(1, 9)
    def _(t):
        dc = column(t)
        arrived_column(pos_copy, dc, True)
        build(dc)

    def column_products(n, dc, picks):
        u = halo[n, dc].astype(f32)
        outs = [None, None]
        for q in picks:
            a, xs = PAIRS[q]
            code = 9 * (xs - a) + 3 * lax.rem(dc, 3) + lax.div(dc, 3)
            weight = weights[a, pl.ds(code, 1), :]
            rows = [u[8 + 24 * xs + 8 * e : 16 + 24 * xs + 8 * e] * weight for e in range(3)]
            term = jnp.dot(
                jnp.concatenate(rows, axis=1).astype(bf16), tiles[dc * 6 + q],
                preferred_element_type=f32,
            )
            outs[a] = term if outs[a] is None else outs[a] + term
        return outs

    def matvec(n, count):
        arrived_column(copies[n], 4, False)
        if count == 9:
            first = column_products(n, 4, range(6))
        else:
            first = column_products(n, 4, (3, 5))

        def step(t, acc):
            dc = column(t)
            arrived_column(copies[n], dc, True)
            outs = column_products(n, dc, range(6))
            return acc[0] + outs[0], acc[1] + outs[1]

        acc = lax.fori_loop(1, count, step, (first[0], first[1]))
        if count < 9:
            home = column_products(n, 4, (1, 4))
            acc = (2.0 * acc[0] + home[0], 2.0 * acc[1] + home[1])
        rows = []
        for a in range(2):
            for c in range(3):
                rows.append(acc[a][:, c * BEAD : (c + 1) * BEAD] * own_mask[a])
        full = jnp.concatenate(rows, axis=0)
        return full - halo[n, 4, MID[0] : MID[0] + MID[1], :].astype(f32)

    def fold(left, right):
        product = left * right
        total = product[0:8]
        for k in range(1, 6):
            total = total + product[8 * k : 8 * k + 8]
        return total

    def homeward(h):
        return (2 * my_x + h, iy, lax.div(my_z, 2))

    current = own[0]
    parts = [fold(current, current)]
    for n in range(2):
        nxt = matvec(n, 9)
        own[n + 1] = nxt
        halo[n + 1, 4, MID[0] : MID[0] + MID[1], :] = nxt.astype(bf16)
        exchange_start(copies[n + 1], 9 if n == 0 else 5)
        for h in range(2):
            move(
                own.at[n + 1, pl.ds(h * CELL, CELL)], back.at[n, lax.rem(my_z, 2)],
                back_send.at[n, h], back_recv.at[n, lax.rem(my_z, 2)], homeward(h),
            )
        parts += [fold(current, nxt), fold(nxt, nxt)]
        current = nxt
    parts.append(fold(current, matvec(2, 5)))

    ones = jnp.ones((SAMPLES, BEAD), f32)
    row = lax.dot_general(
        ones, jnp.concatenate(parts + [jnp.zeros((BEAD - 48, BEAD), f32)], axis=0),
        (((1,), (1,)), ((), ())), precision=lax.Precision.HIGHEST, preferred_element_type=f32,
    )

    def z_copy(k):
        return pltpu.make_async_remote_copy(
            sums_z.at[pl.ds(0, 1)], sums_z.at[pl.ds(k, 1)], z_send.at[k], z_recv.at[k],
            device_id=shifted(0, 0, k), device_id_type=MESH,
        )

    def xy_copy(k):
        return pltpu.make_async_remote_copy(
            sums_xy.at[pl.ds(0, 1)], sums_xy.at[pl.ds(k, 1)], xy_send.at[k], xy_recv.at[k],
            device_id=shifted(lax.div(k, ny), lax.rem(k, ny), 0), device_id_type=MESH,
        )

    def all_sum(buffer, copy, count, value):
        buffer[0:1, :] = value

        @pl.loop(1, count)
        def _(k):
            copy(k).start()

        @pl.loop(1, count)
        def _(k):
            copy(k).wait_recv()

        total = jnp.sum(buffer[...], axis=0, keepdims=True)

        @pl.loop(1, count)
        def _(k):
            copy(k).wait_send()

        return total

    total = all_sum(sums_z, z_copy, nz, row[0:1])
    total = all_sum(sums_xy, xy_copy, nx * ny, total)
    total = jnp.broadcast_to(total, (SAMPLES, BEAD))
    moments = [total] + [pltpu.roll(total, BEAD - 8 * m, 1) for m in range(1, 6)]
    mix = combination(moments)
    for m in range(3):
        row_buf[m : m + 1, :] = mix[m][0:1]
    row_buf[3:8, :] = jnp.zeros((5, BEAD), f32)
    mixed = jnp.transpose(row_buf[...], (1, 0))[0:SAMPLES]

    for n in range(2):
        for b in range(2):
            landed(back.at[n, b], back_recv.at[n, b])
    for b in range(2):
        for c in range(3):
            rows = slice(c * 8, c * 8 + 8)
            out_ref[b, :, c * BEAD : (c + 1) * BEAD] = (
                mixed[:, 0:1] * start_src[b, rows, :]
                + mixed[:, 1:2] * back[0, b, rows, :]
                + mixed[:, 2:3] * back[1, b, rows, :]
            )

    for b in range(2):
        target = device(my_x, iy, 2 * iz + b)
        moved(meta_src.at[b], move_send.at[0, b], target)
        moved(start_src.at[b], move_send.at[1, b], target)
    for n in range(2):
        for h in range(2):
            moved(own.at[n + 1, pl.ds(h * CELL, CELL)], back_send.at[n, h], homeward(h))
    exchange_sent(pos_copy, 9)
    exchange_sent(copies[0], 9)
    exchange_sent(copies[1], 9)
    exchange_sent(copies[2], 5)


def body(positions, block_fill, noise, pair_list, pair_count):
    nx, ny, nz = lax.axis_size("gx") // 2, lax.axis_size("gy"), 2 * lax.axis_size("gz")
    dma = pltpu.SemaphoreType.DMA
    vmem, smem = pl.BlockSpec(memory_space=pltpu.VMEM), pl.BlockSpec(memory_space=pltpu.SMEM)
    out = pl.pallas_call(
        kernel,
        out_shape=jax.ShapeDtypeStruct((2, SAMPLES, 3 * BEAD), f32),
        in_specs=[smem, smem, vmem, vmem, vmem],
        out_specs=vmem,
        scratch_shapes=[
            pltpu.VMEM((2, 8, BEAD), f32),
            pltpu.VMEM((2, CELL, BEAD), f32),
            pltpu.VMEM((9, 4, 8, BEAD), f32),
            pltpu.VMEM((2, CELL, BEAD), f32),
            pltpu.VMEM((3, 9, 112, BEAD), bf16),
            pltpu.VMEM((3, 2 * CELL, BEAD), f32),
            pltpu.VMEM((2, 2, CELL, BEAD), f32),
            pltpu.VMEM((54, 3 * BEAD, 3 * BEAD), bf16),
            pltpu.VMEM((4, BEAD, 8), f32),
            pltpu.VMEM((2, BEAD, BEAD), f32),
            pltpu.VMEM((nz, BEAD), f32),
            pltpu.VMEM((nx * ny, BEAD), f32),
            pltpu.VMEM((8, BEAD), f32),
            dma((2, 2)), dma((2, 2)), dma((2, 2)), dma((2, 2)),
            dma((9, 3)), dma((9, 3)), dma((3, 9, 3)), dma((3, 9, 3)),
            dma((nz,)), dma((nz,)), dma((nx * ny,)), dma((nx * ny,)),
        ],
        compiler_params=pltpu.CompilerParams(
            collective_id=0, has_side_effects=True, vmem_limit_bytes=40 * 1024 * 1024
        ),
    )(
        block_fill.reshape(2), pair_count.reshape(1), pair_list.reshape(3, -1),
        positions.reshape(2, 3, BEAD), noise.reshape(2, SAMPLES, 3 * BEAD),
    )
    return out.reshape(noise.shape)


def solution(mesh):
    cells = P("gx", "gy", "gz", None, None)
    in_specs = (cells, P("gx", "gy", "gz"), cells, cells, P("gx", "gy", "gz"))
    return jax.shard_map(body, mesh=mesh, in_specs=in_specs, out_specs=cells, check_vma=False)
```

```python
import jax
import jax.numpy as jnp
from jax import lax
from jax.experimental import pallas as pl
from jax.experimental.pallas import tpu as pltpu
from jax.sharding import PartitionSpec as P

ROOT_ITERS = 12
RADIUS = 0.08
EPSILON = 1e-6
MESH = pl.DeviceIdType.MESH
BEAD = 128
SAMPLES = 8
CELL = 3 * SAMPLES
LEFT, MID, RIGHT = (0, 32), (32, 48), (80, 32)
PAIRS = ((0, 0), (0, 1), (0, 2), (1, 1), (1, 2), (1, 3))
WIDTH = 3 * BEAD
BLOCKS = ((0, 0), (0, 1), (0, 2), (1, 1), (1, 2), (2, 2))
NEAR_FIRST = (3, 5, 1, 7, 0, 2, 6, 8)
HALF_NEAR = (5, 7, 6, 8)
f32, bf16 = jnp.float32, jnp.bfloat16


def packed(order):
    return sum(dc * 9**t for t, dc in enumerate(order))


def each_column(order, body, carry=0):
    def step(_, state):
        digits, inside = state
        return lax.div(digits, 9), body(lax.rem(digits, 9), inside)

    return lax.fori_loop(0, len(order), step, (jnp.int32(packed(order)), carry))[1]


def tile_factors(d0, d1, d2):
    dist = d0 * d0 + d1 * d1 + d2 * d2
    root = lax.rsqrt(jnp.maximum(dist, 1e-30))
    capped = jnp.minimum(root, 100.0)
    inv = capped * capped
    length = dist * root
    far_iso = capped * (0.75 * RADIUS + (0.5 * RADIUS**3) * inv)
    far_dyad = capped * (0.75 * RADIUS - (1.5 * RADIUS**3) * inv)
    near_iso = 1.0 - (9.0 / 32.0 / RADIUS) * length
    near_dyad = (3.0 / 32.0 / RADIUS) * length
    apart = dist >= 4.0 * RADIUS * RADIUS
    return jnp.where(apart, far_iso, near_iso), jnp.where(apart, far_dyad, near_dyad) * inv


def inverse_three(m):
    def cof(i, j):
        a, b, c, d = (i + 1) % 3, (i + 2) % 3, (j + 1) % 3, (j + 2) % 3
        return m[a][c] * m[b][d] - m[a][d] * m[b][c]

    co = [[cof(i, j) for j in range(3)] for i in range(3)]
    scale = 1.0 / (m[0][0] * co[0][0] + m[0][1] * co[0][1] + m[0][2] * co[0][2])
    return [[co[j][i] * scale for j in range(3)] for i in range(3)]


def combination(moments):
    def inner(left, right):
        total = 0.0
        for i, a in enumerate(left):
            for j, b in enumerate(right):
                total = total + a * b * moments[i + j]
        return total

    def apply(v):
        return [v[0]] + [v[i] + v[i - 1] for i in range(1, len(v))] + [v[-1]]

    norm = jnp.sqrt(moments[0] + EPSILON)
    v1 = [1.0 / norm]
    w1 = apply(v1)
    a1 = inner(v1, w1)
    r1 = [w1[0] - a1 * v1[0], w1[1]]
    b1 = jnp.sqrt(inner(r1, r1) + EPSILON)
    v2 = [r / b1 for r in r1]
    w2 = apply(v2)
    a2 = inner(v2, w2)
    r2 = [w2[0] - a2 * v2[0] - b1 * v1[0], w2[1] - a2 * v2[1], w2[2]]
    b2 = jnp.sqrt(inner(r2, r2) + EPSILON)
    v3 = [r / b2 for r in r2]
    a3 = inner(v3, apply(v3))
    scale = (a1 + a2 + a3) / 3.0
    zero, one = jnp.zeros_like(a1), jnp.ones_like(a1)
    y = [[e / scale for e in row] for row in ((a1, b1, zero), (b1, a2, b2), (zero, b2, a3))]
    z = [[one if i == j else zero for j in range(3)] for i in range(3)]

    def step(_, state):
        y, z = state
        iz, iy = inverse_three(z), inverse_three(y)
        return (
            [[0.5 * (y[i][j] + iz[i][j]) for j in range(3)] for i in range(3)],
            [[0.5 * (z[i][j] + iy[i][j]) for j in range(3)] for i in range(3)],
        )

    y, z = lax.fori_loop(0, ROOT_ITERS, step, (y, z))
    root = [jnp.sqrt(scale) * y[i][0] for i in range(3)]
    return [
        norm * (root[0] * v1[0] + root[1] * v2[0] + root[2] * v3[0]),
        norm * (root[1] * v2[1] + root[2] * v3[1]),
        norm * (root[2] * v3[2]),
    ]


def kernel(
    fill_hbm, count_hbm, list_hbm, pos_hbm, noise_hbm, out_ref,
    fill_ref, count_ref, list_ref, pos_ref, noise_ref, meta_src, start_src, pos_halo, start_own, halo, own, back, tiles, columns, weights,
    sums_z, sums_xy, row_buf,
    input_sem, move_send, move_recv, back_send, back_recv, pos_send, pos_recv, u_send, u_recv,
    z_send, z_recv, xy_send, xy_recv,
):
    ix, iy, iz = lax.axis_index("gx"), lax.axis_index("gy"), lax.axis_index("gz")
    nx = lax.axis_size("gx") // 2
    ny = lax.axis_size("gy")
    half = lax.axis_size("gz")
    nz = 2 * half
    my_x, my_z = lax.div(ix, 2), lax.rem(ix, 2) * half + iz

    def device(x, y, z):
        return (2 * x + lax.div(z, half), y, lax.rem(z, half))

    def shifted(dx, dy, dz):
        return device(
            lax.rem(my_x + dx + nx, nx), lax.rem(iy + dy + ny, ny), lax.rem(my_z + dz + nz, nz)
        )

    inputs = [
        pltpu.make_async_copy(src, dst, input_sem.at[k])
        for k, (src, dst) in enumerate(
            (
                (fill_hbm, fill_ref), (count_hbm, count_ref), (list_hbm, list_ref),
                (pos_hbm, pos_ref), (noise_hbm, noise_ref),
            )
        )
    ]
    for copy in inputs:
        copy.start()

    barrier = pltpu.get_barrier_semaphore()

    def greet(dx, dy, dz):
        pl.semaphore_signal(barrier, inc=1, device_id=shifted(dx, dy, dz), device_id_type=MESH)

    @pl.loop(1, nz)
    def _(k):
        greet(0, 0, k)

    @pl.loop(1, nx * ny)
    def _(k):
        greet(lax.div(k, ny), lax.rem(k, ny), 0)

    @pl.loop(0, 16)
    def _(k):
        q = lax.rem(k, 8)
        q = q + lax.div(q + 4, 8)
        greet(lax.div(q, 3) - 1, lax.rem(q, 3) - 1, 2 * lax.div(k, 8) - 1)

    lanes = lax.broadcasted_iota(jnp.int32, (1, BEAD), 1)
    slots = list_ref.shape[2]
    for copy in inputs:
        copy.wait()
    codes = lax.broadcasted_iota(jnp.int32, (BEAD, slots), 0)
    live = lax.broadcasted_iota(jnp.int32, (1, slots), 1) < count_ref[0:1, 0:1]
    chosen = jnp.where(codes == list_ref[1], 1.0, 0.0).astype(bf16)
    masks = []
    for b in range(2):
        mask = jnp.where(lanes < fill_ref[0:1, b : b + 1], 1.0, 0.0)
        masks.append(mask)
        here = jnp.where(live & (list_ref[0] == b), 1.0, 0.0)
        here = jnp.broadcast_to(here, (SAMPLES, slots)).astype(bf16)
        tally = lax.dot_general(
            here, chosen, (((1,), (1,)), ((), ())), preferred_element_type=f32
        )
        for c in range(3):
            meta_src[b, c : c + 1, :] = pos_ref[c, b : b + 1, :]
        meta_src[b, 3:4, :] = mask
        meta_src[b, 4:5, :] = tally[0:1]
        meta_src[b, 5:8, :] = jnp.zeros((3, BEAD), f32)
        for c in range(3):
            start_src[b, c * 8 : c * 8 + 8, :] = noise_ref[b, :, c * BEAD : (c + 1) * BEAD] * mask

    pl.semaphore_wait(barrier, (nz - 1) + (nx * ny - 1) + 16)

    def move(src, dst, send, recv, target):
        tx, ty, tz = target
        same = (tx == ix) & (tz == iz)

        @pl.when(same)
        def _():
            pltpu.make_async_copy(src, dst, recv).start()

        @pl.when(jnp.logical_not(same))
        def _():
            pltpu.make_async_remote_copy(
                src, dst, send, recv, device_id=target, device_id_type=MESH
            ).start()

    def moved(src, send, target):
        tx, ty, tz = target
        same = (tx == ix) & (tz == iz)

        @pl.when(jnp.logical_not(same))
        def _():
            pltpu.make_async_remote_copy(
                src, src, send, send, device_id=target, device_id_type=MESH
            ).wait_send()

    def landed(dst, recv):
        pltpu.make_async_copy(dst, dst, recv).wait()

    side = lax.rem(ix, 2)
    for b in range(2):
        target = device(my_x, iy, 2 * iz + b)
        move(meta_src.at[b], pos_halo.at[4, 1 + side], move_send.at[0, b], move_recv.at[0, side], target)
    for b in range(2):
        target = device(my_x, iy, 2 * iz + b)
        move(start_src.at[b], start_own.at[side], move_send.at[1, b], move_recv.at[1, side], target)
    for h in range(2):
        landed(pos_halo.at[4, 1 + h], move_recv.at[0, h])

    def exchange(src_of, dst_of, column_of, send, recv):
        def copy(dc, part, dx):
            side_sem = 1 if isinstance(dc, int) else 0
            dy, dz = 1 - lax.rem(dc, 3), 1 - lax.div(dc, 3)
            return pltpu.make_async_remote_copy(
                src_of(part), dst_of(dc, part), send.at[side_sem], recv.at[dc],
                device_id=shifted(dx, dy, dz), device_id_type=MESH,
            )

        def start(order):
            def step(dc, carry):
                copy(dc, 0, 1).start()
                copy(dc, 2, -1).start()
                copy(dc, 1, 0).start()
                return carry

            each_column(order, step)
            copy(4, 0, 1).start()
            copy(4, 2, -1).start()

        def sent(order):
            bytes_of = column_of(slice(0, len(order)))
            pltpu.make_async_copy(bytes_of, bytes_of, send.at[0]).wait()
            sides = dst_of(4, 3)
            pltpu.make_async_copy(sides, sides, send.at[1]).wait()

        def arrived(dc):
            if isinstance(dc, int) and dc == 4:
                sides = dst_of(4, 3)
                pltpu.make_async_copy(sides, sides, recv.at[4]).wait()
            else:
                whole = column_of(dc)
                pltpu.make_async_copy(whole, whole, recv.at[dc]).wait()

        return start, sent, arrived

    def columns_of(ref, dc):
        return ref.at[pl.ds(0, dc.stop)] if isinstance(dc, slice) else ref.at[dc]

    pos_src = {0: (2, 1), 1: (1, 2), 2: (1, 1)}
    pos_dst = {0: (0, 1), 1: (1, 2), 2: (3, 1), 3: (0, 2)}
    pos_start, pos_sent, pos_arrived = exchange(
        lambda part: pos_halo.at[4, pl.ds(*pos_src[part])],
        lambda dc, part: pos_halo.at[dc, pl.ds(*pos_dst[part])],
        lambda dc: columns_of(pos_halo, dc), pos_send, pos_recv,
    )
    pos_start(NEAR_FIRST)

    own_mask = []
    for h in range(2):
        own_mask.append(pos_halo[4, 1 + h, 3:4, :])
        table = jnp.transpose(pos_halo[4, 1 + h], (1, 0))
        weights[h] = jnp.broadcast_to(table[:, 4:5], (BEAD, BEAD))

    u_src = {0: (48, 32), 1: (32, 48), 2: (32, 32)}
    u_dst = {0: LEFT, 1: MID, 2: RIGHT, 3: (0, 64)}

    def u_copy(n):
        return exchange(
            lambda part: halo.at[n, 4, pl.ds(*u_src[part])],
            lambda dc, part: halo.at[n, dc, pl.ds(*u_dst[part])],
            lambda dc: columns_of(halo.at[n], dc), u_send.at[n], u_recv.at[n],
        )

    copies = [u_copy(n) for n in range(3)]
    for h in range(2):
        landed(start_own.at[h], move_recv.at[1, h])
    start = jnp.concatenate([start_own[0], start_own[1]], axis=0)
    own[0] = start
    halo[0, 4, MID[0] : MID[0] + MID[1], :] = start.astype(bf16)
    copies[0][0](NEAR_FIRST)

    def build(dc):
        for xs in range(4):
            columns[xs] = jnp.transpose(pos_halo[dc, xs], (1, 0))
        mine = [[pos_halo[4, 1 + a, c : c + 1, :] for c in range(3)] for a in range(2)]

        @pl.loop(0, BEAD // 16, unroll=8)
        def _(r):
            row = pl.multiple_of(r * 16, 16)
            away = []
            for xs in range(4):
                block = columns[xs, pl.ds(row, 16), :]
                away.append(
                    [jnp.broadcast_to(block[:, c : c + 1], (16, BEAD)) for c in range(3)]
                )
            for q, (a, xs) in enumerate(PAIRS):
                d = [away[xs][c] - mine[a][c] for c in range(3)]
                iso, dyad = tile_factors(*d)
                scaled = [dyad * d[c] for c in range(3)]
                for k, (c, e) in enumerate(BLOCKS):
                    entry = scaled[c] * d[e]
                    entry = entry + iso if c == e else entry
                    tiles[dc, q, k, pl.ds(row, 16), :] = entry.astype(bf16)

    def products(n, a, dc, first, count):
        entries, blocks = [], []
        u = halo[n, dc].astype(f32)
        row, deep = (dc % 3, dc // 3) if isinstance(dc, int) else (lax.rem(dc, 3), lax.div(dc, 3))
        for xs in range(a + first, a + first + count):
            weight = weights[a, pl.ds(9 * (xs - a) + 3 * row + deep, 1), :]
            for e in range(3):
                entries.append(u[8 + 24 * xs + 8 * e : 16 + 24 * xs + 8 * e] * weight)
                parts = [
                    tiles[dc, 2 * a + xs, BLOCKS.index((min(c, e), max(c, e)))] for c in range(3)
                ]
                blocks.append(jnp.concatenate(parts, axis=1))
        return jnp.dot(
            jnp.concatenate(entries, axis=1).astype(bf16),
            jnp.concatenate(blocks, axis=0),
            preferred_element_type=f32,
        )

    pos_arrived(4)
    build(4)
    copies[0][2](4)

    def build_next(dc, state):
        before, left, right = state
        pos_arrived(dc)
        left = left + products(0, 0, before, 0, 3)
        right = right + products(0, 1, before, 0, 3)
        build(dc)
        copies[0][2](dc)
        return dc, left, right

    blank = jnp.zeros((SAMPLES, WIDTH), f32)
    state = each_column(NEAR_FIRST, build_next, (jnp.int32(4), blank, blank))
    image = [state[1 + a] + products(0, a, state[0], 0, 3) for a in range(2)]

    def matvec(n):
        arrived = copies[n][2]
        if n == 0:
            acc = image
        elif n == 1:
            acc = [0.0, 0.0]
            for dc in (4, *NEAR_FIRST):
                arrived(dc)
                acc = [acc[a] + products(n, a, dc, 0, 3) for a in range(2)]
        else:
            arrived(4)
            acc = [products(n, a, 4, 2, 1) for a in range(2)]
            for dc in HALF_NEAR:
                arrived(dc)
                acc = [acc[a] + products(n, a, dc, 0, 3) for a in range(2)]
            acc = [2.0 * acc[a] + products(n, a, 4, 1, 1) for a in range(2)]
        rows = []
        for a in range(2):
            for c in range(3):
                rows.append(acc[a][:, c * BEAD : (c + 1) * BEAD] * own_mask[a])
        full = jnp.concatenate(rows, axis=0)
        return full - halo[n, 4, MID[0] : MID[0] + MID[1], :].astype(f32)

    def fold(left, right):
        product = left * right
        total = product[0:8]
        for k in range(1, 6):
            total = total + product[8 * k : 8 * k + 8]
        return total

    def homeward(h):
        return (2 * my_x + h, iy, lax.div(my_z, 2))

    current = own[0]
    parts = [fold(current, current)]
    for n in range(2):
        nxt = matvec(n)
        own[n + 1] = nxt
        halo[n + 1, 4, MID[0] : MID[0] + MID[1], :] = nxt.astype(bf16)
        copies[n + 1][0](NEAR_FIRST if n == 0 else HALF_NEAR)
        for h in range(2):
            move(
                own.at[n + 1, pl.ds(h * CELL, CELL)], back.at[n, lax.rem(my_z, 2)],
                back_send.at[n, h], back_recv.at[n, lax.rem(my_z, 2)], homeward(h),
            )
        parts += [fold(current, nxt), fold(nxt, nxt)]
        current = nxt
        copies[n][1](NEAR_FIRST)
        if n == 0:
            pos_sent(NEAR_FIRST)
            for b in range(2):
                target = device(my_x, iy, 2 * iz + b)
                moved(meta_src.at[b], move_send.at[0, b], target)
                moved(start_src.at[b], move_send.at[1, b], target)
    parts.append(fold(current, matvec(2)))

    ones = jnp.ones((SAMPLES, BEAD), f32)
    row = lax.dot_general(
        ones, jnp.concatenate(parts + [jnp.zeros((BEAD - 48, BEAD), f32)], axis=0),
        (((1,), (1,)), ((), ())), precision=lax.Precision.HIGHEST, preferred_element_type=f32,
    )

    def all_sum(buffer, send, recv, count, shift, value, between):
        buffer[0:1, :] = value

        @pl.loop(1, count)
        def _(k):
            pltpu.make_async_remote_copy(
                buffer.at[pl.ds(0, 1)], buffer.at[pl.ds(k, 1)], send, recv,
                device_id=shift(k), device_id_type=MESH,
            ).start()

        between()
        others = buffer.at[pl.ds(1, count - 1)]
        pltpu.make_async_copy(others, others, recv).wait()
        return jnp.sum(buffer[...], axis=0, keepdims=True)

    def all_sent(buffer, send, count):
        others = buffer.at[pl.ds(1, count - 1)]
        pltpu.make_async_copy(others, others, send).wait()

    def tidy_halo():
        copies[2][1](HALF_NEAR)
        for n in range(2):
            for h in range(2):
                moved(own.at[n + 1, pl.ds(h * CELL, CELL)], back_send.at[n, h], homeward(h))

    def tidy_back():
        for n in range(2):
            for b in range(2):
                landed(back.at[n, b], back_recv.at[n, b])
        all_sent(sums_z, z_send, nz)

    total = all_sum(sums_z, z_send, z_recv, nz, lambda k: shifted(0, 0, k), row[0:1], tidy_halo)
    total = all_sum(
        sums_xy, xy_send, xy_recv, nx * ny,
        lambda k: shifted(lax.div(k, ny), lax.rem(k, ny), 0), total, tidy_back,
    )
    total = jnp.broadcast_to(total, (SAMPLES, BEAD))
    moments = [total] + [pltpu.roll(total, BEAD - 8 * m, 1) for m in range(1, 6)]
    mix = combination(moments)
    for m in range(3):
        row_buf[m : m + 1, :] = mix[m][0:1]
    row_buf[3:8, :] = jnp.zeros((5, BEAD), f32)
    mixed = jnp.transpose(row_buf[...], (1, 0))[0:SAMPLES]

    for b in range(2):
        for c in range(3):
            rows = slice(c * 8, c * 8 + 8)
            out_ref[b, :, c * BEAD : (c + 1) * BEAD] = (
                mixed[:, 0:1] * start_src[b, rows, :]
                + mixed[:, 1:2] * back[0, b, rows, :]
                + mixed[:, 2:3] * back[1, b, rows, :]
            )

    all_sent(sums_xy, xy_send, nx * ny)


def body(positions, block_fill, noise, pair_list, pair_count):
    nx, ny, nz = lax.axis_size("gx") // 2, lax.axis_size("gy"), 2 * lax.axis_size("gz")
    dma = pltpu.SemaphoreType.DMA
    vmem, hbm = pl.BlockSpec(memory_space=pltpu.VMEM), pl.BlockSpec(memory_space=pltpu.HBM)
    slots = pair_list.shape[-1]
    out = pl.pallas_call(
        kernel,
        out_shape=jax.ShapeDtypeStruct((2, SAMPLES, 3 * BEAD), f32),
        in_specs=[hbm] * 5,
        out_specs=vmem,
        scratch_shapes=[
            pltpu.VMEM((1, 2), jnp.int32),
            pltpu.VMEM((1, 1), jnp.int32),
            pltpu.VMEM((3, 1, slots), jnp.int32),
            pltpu.VMEM((3, 2, BEAD), f32),
            pltpu.VMEM((2, SAMPLES, WIDTH), f32),
            pltpu.VMEM((2, 8, BEAD), f32),
            pltpu.VMEM((2, CELL, BEAD), f32),
            pltpu.VMEM((9, 4, 8, BEAD), f32),
            pltpu.VMEM((2, CELL, BEAD), f32),
            pltpu.VMEM((3, 9, 112, BEAD), bf16),
            pltpu.VMEM((3, 2 * CELL, BEAD), f32),
            pltpu.VMEM((2, 2, CELL, BEAD), f32),
            pltpu.VMEM((9, 6, 6, BEAD, BEAD), bf16),
            pltpu.VMEM((4, BEAD, 8), f32),
            pltpu.VMEM((2, BEAD, BEAD), f32),
            pltpu.VMEM((nz, BEAD), f32),
            pltpu.VMEM((nx * ny, BEAD), f32),
            pltpu.VMEM((8, BEAD), f32),
            dma((5,)), dma((2, 2)), dma((2, 2)), dma((2, 2)), dma((2, 2)),
            dma((2,)), dma((9,)), dma((3, 2)), dma((3, 9)), dma, dma, dma, dma,
        ],
        compiler_params=pltpu.CompilerParams(
            collective_id=0, has_side_effects=True, vmem_limit_bytes=60 * 1024 * 1024
        ),
    )(
        block_fill.reshape(1, 2), pair_count.reshape(1, 1), pair_list.reshape(3, 1, slots),
        positions.reshape(2, 3, BEAD).transpose(1, 0, 2), noise.reshape(2, SAMPLES, 3 * BEAD),
    )
    return out.reshape(noise.shape)


def solution(mesh):
    cells = P("gx", "gy", "gz", None, None)
    in_specs = (cells, P("gx", "gy", "gz"), cells, cells, P("gx", "gy", "gz"))
    return jax.shard_map(body, mesh=mesh, in_specs=in_specs, out_specs=cells, check_vma=False)
```

```python
import jax
import jax.numpy as jnp
from jax import lax
from jax.experimental import pallas as pl
from jax.experimental.pallas import tpu as pltpu
from jax.sharding import PartitionSpec as P

ROOT_ITERS = 12
RADIUS = 0.08
EPSILON = 1e-6
MESH = pl.DeviceIdType.MESH
BEAD = 128
SAMPLES = 8
CELL = 3 * SAMPLES
LEFT, MID, RIGHT = (0, 32), (32, 48), (80, 32)
PAIRS = ((0, 0), (0, 1), (0, 2), (1, 1), (1, 2), (1, 3))
WIDTH = 3 * BEAD
BLOCKS = ((0, 0), (0, 1), (0, 2), (1, 1), (1, 2), (2, 2))
NEAR_FIRST = (3, 5, 1, 7, 0, 2, 6, 8)
HALF_NEAR = (5, 7, 6, 8)
f32, bf16 = jnp.float32, jnp.bfloat16


def packed(order):
    return sum(dc * 9**t for t, dc in enumerate(order))


def each_column(order, body, carry=0):
    def step(_, state):
        digits, inside = state
        return lax.div(digits, 9), body(lax.rem(digits, 9), inside)

    return lax.fori_loop(0, len(order), step, (jnp.int32(packed(order)), carry))[1]


def tile_factors(d0, d1, d2):
    dist = d0 * d0 + d1 * d1 + d2 * d2
    root = lax.rsqrt(jnp.maximum(dist, 1e-30))
    capped = jnp.minimum(root, 100.0)
    inv = capped * capped
    length = dist * root
    far_iso = capped * (0.75 * RADIUS + (0.5 * RADIUS**3) * inv)
    far_dyad = capped * (0.75 * RADIUS - (1.5 * RADIUS**3) * inv)
    near_iso = 1.0 - (9.0 / 32.0 / RADIUS) * length
    near_dyad = (3.0 / 32.0 / RADIUS) * length
    apart = dist >= 4.0 * RADIUS * RADIUS
    return jnp.where(apart, far_iso, near_iso), jnp.where(apart, far_dyad, near_dyad) * inv


def inverse_three(m):
    def cof(i, j):
        a, b, c, d = (i + 1) % 3, (i + 2) % 3, (j + 1) % 3, (j + 2) % 3
        return m[a][c] * m[b][d] - m[a][d] * m[b][c]

    co = [[cof(i, j) for j in range(3)] for i in range(3)]
    scale = 1.0 / (m[0][0] * co[0][0] + m[0][1] * co[0][1] + m[0][2] * co[0][2])
    return [[co[j][i] * scale for j in range(3)] for i in range(3)]


def combination(moments):
    def inner(left, right):
        total = 0.0
        for i, a in enumerate(left):
            for j, b in enumerate(right):
                total = total + a * b * moments[i + j]
        return total

    def apply(v):
        return [v[0]] + [v[i] + v[i - 1] for i in range(1, len(v))] + [v[-1]]

    norm = jnp.sqrt(moments[0] + EPSILON)
    v1 = [1.0 / norm]
    w1 = apply(v1)
    a1 = inner(v1, w1)
    r1 = [w1[0] - a1 * v1[0], w1[1]]
    b1 = jnp.sqrt(inner(r1, r1) + EPSILON)
    v2 = [r / b1 for r in r1]
    w2 = apply(v2)
    a2 = inner(v2, w2)
    r2 = [w2[0] - a2 * v2[0] - b1 * v1[0], w2[1] - a2 * v2[1], w2[2]]
    b2 = jnp.sqrt(inner(r2, r2) + EPSILON)
    v3 = [r / b2 for r in r2]
    a3 = inner(v3, apply(v3))
    scale = (a1 + a2 + a3) / 3.0
    zero, one = jnp.zeros_like(a1), jnp.ones_like(a1)
    y = [[e / scale for e in row] for row in ((a1, b1, zero), (b1, a2, b2), (zero, b2, a3))]
    z = [[one if i == j else zero for j in range(3)] for i in range(3)]

    def step(_, state):
        y, z = state
        iz, iy = inverse_three(z), inverse_three(y)
        return (
            [[0.5 * (y[i][j] + iz[i][j]) for j in range(3)] for i in range(3)],
            [[0.5 * (z[i][j] + iy[i][j]) for j in range(3)] for i in range(3)],
        )

    y, z = lax.fori_loop(0, ROOT_ITERS, step, (y, z))
    root = [jnp.sqrt(scale) * y[i][0] for i in range(3)]
    return [
        norm * (root[0] * v1[0] + root[1] * v2[0] + root[2] * v3[0]),
        norm * (root[1] * v2[1] + root[2] * v3[1]),
        norm * (root[2] * v3[2]),
    ]


def kernel(
    fill_hbm, count_hbm, list_hbm, pos_hbm, noise_hbm, out_ref,
    fill_ref, count_ref, list_ref, pos_ref, noise_ref, meta_src, start_src, pos_halo, start_own, halo, own, back, tiles, columns, weights,
    sums_z, sums_xy, row_buf,
    input_sem, move_send, move_recv, back_send, back_recv, pos_send, pos_recv, u_send, u_recv,
    z_send, z_recv, xy_send, xy_recv,
):
    ix, iy, iz = lax.axis_index("gx"), lax.axis_index("gy"), lax.axis_index("gz")
    nx = lax.axis_size("gx") // 2
    ny = lax.axis_size("gy")
    half = lax.axis_size("gz")
    nz = 2 * half
    turn = nz // 4
    my_x, my_z = lax.div(ix, 2), lax.rem(lax.rem(ix, 2) * half + iz + turn, nz)

    def device(x, y, z):
        place = lax.rem(z + nz - turn, nz)
        return (2 * x + lax.div(place, half), y, lax.rem(place, half))

    def shifted(dx, dy, dz):
        return device(
            lax.rem(my_x + dx + nx, nx), lax.rem(iy + dy + ny, ny), lax.rem(my_z + dz + nz, nz)
        )

    inputs = [
        pltpu.make_async_copy(src, dst, input_sem.at[k])
        for k, (src, dst) in enumerate(
            (
                (fill_hbm, fill_ref), (count_hbm, count_ref), (list_hbm, list_ref),
                (pos_hbm, pos_ref), (noise_hbm, noise_ref),
            )
        )
    ]
    for copy in inputs:
        copy.start()

    barrier = pltpu.get_barrier_semaphore()

    def greet(dx, dy, dz):
        pl.semaphore_signal(barrier, inc=1, device_id=shifted(dx, dy, dz), device_id_type=MESH)

    @pl.loop(1, nz)
    def _(k):
        greet(0, 0, k)

    @pl.loop(1, nx * ny)
    def _(k):
        greet(lax.div(k, ny), lax.rem(k, ny), 0)

    @pl.loop(0, 16)
    def _(k):
        q = lax.rem(k, 8)
        q = q + lax.div(q + 4, 8)
        greet(lax.div(q, 3) - 1, lax.rem(q, 3) - 1, 2 * lax.div(k, 8) - 1)

    lanes = lax.broadcasted_iota(jnp.int32, (1, BEAD), 1)
    slots = list_ref.shape[2]
    for copy in inputs:
        copy.wait()
    codes = lax.broadcasted_iota(jnp.int32, (BEAD, slots), 0)
    live = lax.broadcasted_iota(jnp.int32, (1, slots), 1) < count_ref[0:1, 0:1]
    chosen = jnp.where(codes == list_ref[1], 1.0, 0.0).astype(bf16)
    masks = []
    for b in range(2):
        mask = jnp.where(lanes < fill_ref[0:1, b : b + 1], 1.0, 0.0)
        masks.append(mask)
        here = jnp.where(live & (list_ref[0] == b), 1.0, 0.0)
        here = jnp.broadcast_to(here, (SAMPLES, slots)).astype(bf16)
        tally = lax.dot_general(
            here, chosen, (((1,), (1,)), ((), ())), preferred_element_type=f32
        )
        for c in range(3):
            meta_src[b, c : c + 1, :] = pos_ref[c, b : b + 1, :]
        meta_src[b, 3:4, :] = mask
        meta_src[b, 4:5, :] = tally[0:1]
        meta_src[b, 5:8, :] = jnp.zeros((3, BEAD), f32)
        for c in range(3):
            start_src[b, c * 8 : c * 8 + 8, :] = noise_ref[b, :, c * BEAD : (c + 1) * BEAD] * mask

    pl.semaphore_wait(barrier, (nz - 1) + (nx * ny - 1) + 16)

    def move(src, dst, send, recv, target):
        tx, ty, tz = target
        same = (tx == ix) & (tz == iz)

        @pl.when(same)
        def _():
            pltpu.make_async_copy(src, dst, recv).start()

        @pl.when(jnp.logical_not(same))
        def _():
            pltpu.make_async_remote_copy(
                src, dst, send, recv, device_id=target, device_id_type=MESH
            ).start()

    def moved(src, send, target):
        tx, ty, tz = target
        same = (tx == ix) & (tz == iz)

        @pl.when(jnp.logical_not(same))
        def _():
            pltpu.make_async_remote_copy(
                src, src, send, send, device_id=target, device_id_type=MESH
            ).wait_send()

    def landed(dst, recv):
        pltpu.make_async_copy(dst, dst, recv).wait()

    side = lax.rem(ix, 2)
    for b in range(2):
        target = device(my_x, iy, 2 * iz + b)
        move(meta_src.at[b], pos_halo.at[4, 1 + side], move_send.at[0, b], move_recv.at[0, side], target)
    for b in range(2):
        target = device(my_x, iy, 2 * iz + b)
        move(start_src.at[b], start_own.at[side], move_send.at[1, b], move_recv.at[1, side], target)
    for h in range(2):
        landed(pos_halo.at[4, 1 + h], move_recv.at[0, h])

    def exchange(src_of, dst_of, column_of, send, recv):
        def copy(dc, part, dx):
            side_sem = 1 if isinstance(dc, int) else 0
            dy, dz = 1 - lax.rem(dc, 3), 1 - lax.div(dc, 3)
            return pltpu.make_async_remote_copy(
                src_of(part), dst_of(dc, part), send.at[side_sem], recv.at[dc],
                device_id=shifted(dx, dy, dz), device_id_type=MESH,
            )

        def start(order):
            def step(dc, carry):
                copy(dc, 0, 1).start()
                copy(dc, 2, -1).start()
                copy(dc, 1, 0).start()
                return carry

            each_column(order, step)
            copy(4, 0, 1).start()
            copy(4, 2, -1).start()

        def sent(order):
            bytes_of = column_of(slice(0, len(order)))
            pltpu.make_async_copy(bytes_of, bytes_of, send.at[0]).wait()
            sides = dst_of(4, 3)
            pltpu.make_async_copy(sides, sides, send.at[1]).wait()

        def arrived(dc):
            if isinstance(dc, int) and dc == 4:
                sides = dst_of(4, 3)
                pltpu.make_async_copy(sides, sides, recv.at[4]).wait()
            else:
                whole = column_of(dc)
                pltpu.make_async_copy(whole, whole, recv.at[dc]).wait()

        return start, sent, arrived

    def columns_of(ref, dc):
        return ref.at[pl.ds(0, dc.stop)] if isinstance(dc, slice) else ref.at[dc]

    pos_src = {0: (2, 1), 1: (1, 2), 2: (1, 1)}
    pos_dst = {0: (0, 1), 1: (1, 2), 2: (3, 1), 3: (0, 2)}
    pos_start, pos_sent, pos_arrived = exchange(
        lambda part: pos_halo.at[4, pl.ds(*pos_src[part])],
        lambda dc, part: pos_halo.at[dc, pl.ds(*pos_dst[part])],
        lambda dc: columns_of(pos_halo, dc), pos_send, pos_recv,
    )
    pos_start(NEAR_FIRST)

    own_mask = []
    for h in range(2):
        own_mask.append(pos_halo[4, 1 + h, 3:4, :])
        table = jnp.transpose(pos_halo[4, 1 + h], (1, 0))
        weights[h] = jnp.broadcast_to(table[:, 4:5], (BEAD, BEAD))

    u_src = {0: (48, 32), 1: (32, 48), 2: (32, 32)}
    u_dst = {0: LEFT, 1: MID, 2: RIGHT, 3: (0, 64)}

    def u_copy(n):
        return exchange(
            lambda part: halo.at[n, 4, pl.ds(*u_src[part])],
            lambda dc, part: halo.at[n, dc, pl.ds(*u_dst[part])],
            lambda dc: columns_of(halo.at[n], dc), u_send.at[n], u_recv.at[n],
        )

    copies = [u_copy(n) for n in range(3)]
    for h in range(2):
        landed(start_own.at[h], move_recv.at[1, h])
    start = jnp.concatenate([start_own[0], start_own[1]], axis=0)
    own[0] = start
    halo[0, 4, MID[0] : MID[0] + MID[1], :] = start.astype(bf16)
    copies[0][0](NEAR_FIRST)

    def build(dc, pairs=(0, 1, 2, 3, 4, 5)):
        for xs in sorted({PAIRS[q][1] for q in pairs}):
            columns[xs] = jnp.transpose(pos_halo[dc, xs], (1, 0))
        mine = [[pos_halo[4, 1 + a, c : c + 1, :] for c in range(3)] for a in range(2)]

        @pl.loop(0, BEAD // 16, unroll=8)
        def _(r):
            row = pl.multiple_of(r * 16, 16)
            away = {}
            for xs in sorted({PAIRS[q][1] for q in pairs}):
                block = columns[xs, pl.ds(row, 16), :]
                away[xs] = [jnp.broadcast_to(block[:, c : c + 1], (16, BEAD)) for c in range(3)]
            for q in pairs:
                a, xs = PAIRS[q]
                d = [away[xs][c] - mine[a][c] for c in range(3)]
                iso, dyad = tile_factors(*d)
                scaled = [dyad * d[c] for c in range(3)]
                for k, (c, e) in enumerate(BLOCKS):
                    entry = scaled[c] * d[e]
                    entry = entry + iso if c == e else entry
                    tiles[dc, q, k, pl.ds(row, 16), :] = entry.astype(bf16)

    def products(n, a, dc, first, count):
        entries, blocks = [], []
        u = halo[n, dc].astype(f32)
        row, deep = (dc % 3, dc // 3) if isinstance(dc, int) else (lax.rem(dc, 3), lax.div(dc, 3))
        for xs in range(a + first, a + first + count):
            weight = weights[a, pl.ds(9 * (xs - a) + 3 * row + deep, 1), :]
            for e in range(3):
                entries.append(u[8 + 24 * xs + 8 * e : 16 + 24 * xs + 8 * e] * weight)
                parts = [
                    tiles[dc, 2 * a + xs, BLOCKS.index((min(c, e), max(c, e)))] for c in range(3)
                ]
                blocks.append(jnp.concatenate(parts, axis=1))
        total = None
        for x in range(count):
            left = jnp.concatenate(entries[3 * x : 3 * x + 3], axis=1).astype(bf16)
            right = jnp.concatenate(blocks[3 * x : 3 * x + 3], axis=0)
            term = jnp.dot(left, right, preferred_element_type=f32)
            total = term if total is None else total + term
        return total

    build(4, (1, 2, 3, 4))
    pos_arrived(4)
    build(4, (0, 5))
    copies[0][2](4)

    def build_next(dc, state):
        before, left, right = state
        pos_arrived(dc)
        left = left + products(0, 0, before, 0, 3)
        right = right + products(0, 1, before, 0, 3)
        build(dc)
        copies[0][2](dc)
        return dc, left, right

    blank = jnp.zeros((SAMPLES, WIDTH), f32)
    state = each_column(NEAR_FIRST, build_next, (jnp.int32(4), blank, blank))
    image = [state[1 + a] + products(0, a, state[0], 0, 3) for a in range(2)]

    def matvec(n):
        arrived = copies[n][2]
        if n == 0:
            acc = image
        elif n == 1:
            acc = [0.0, 0.0]
            for dc in (4, *NEAR_FIRST):
                arrived(dc)
                acc = [acc[a] + products(n, a, dc, 0, 3) for a in range(2)]
        else:
            arrived(4)
            acc = [products(n, a, 4, 2, 1) for a in range(2)]
            for dc in HALF_NEAR:
                arrived(dc)
                acc = [acc[a] + products(n, a, dc, 0, 3) for a in range(2)]
            acc = [2.0 * acc[a] + products(n, a, 4, 1, 1) for a in range(2)]
        rows = []
        for a in range(2):
            for c in range(3):
                rows.append(acc[a][:, c * BEAD : (c + 1) * BEAD] * own_mask[a])
        full = jnp.concatenate(rows, axis=0)
        return full - halo[n, 4, MID[0] : MID[0] + MID[1], :].astype(f32)

    def fold(left, right):
        product = left * right
        total = product[0:8]
        for k in range(1, 6):
            total = total + product[8 * k : 8 * k + 8]
        return total

    def homeward(h):
        return (2 * my_x + h, iy, lax.div(my_z, 2))

    current = own[0]
    parts = [fold(current, current)]
    for n in range(2):
        nxt = matvec(n)
        own[n + 1] = nxt
        halo[n + 1, 4, MID[0] : MID[0] + MID[1], :] = nxt.astype(bf16)
        copies[n + 1][0](NEAR_FIRST if n == 0 else HALF_NEAR)
        for h in range(2):
            move(
                own.at[n + 1, pl.ds(h * CELL, CELL)], back.at[n, lax.rem(my_z, 2)],
                back_send.at[n, h], back_recv.at[n, lax.rem(my_z, 2)], homeward(h),
            )
        parts += [fold(current, nxt), fold(nxt, nxt)]
        current = nxt
        copies[n][1](NEAR_FIRST)
        if n == 0:
            pos_sent(NEAR_FIRST)
            for b in range(2):
                target = device(my_x, iy, 2 * iz + b)
                moved(meta_src.at[b], move_send.at[0, b], target)
                moved(start_src.at[b], move_send.at[1, b], target)
    parts.append(fold(current, matvec(2)))

    ones = jnp.ones((SAMPLES, BEAD), f32)
    row = lax.dot_general(
        ones, jnp.concatenate(parts + [jnp.zeros((BEAD - 48, BEAD), f32)], axis=0),
        (((1,), (1,)), ((), ())), precision=lax.Precision.HIGHEST, preferred_element_type=f32,
    )

    def all_sum(buffer, send, recv, count, shift, value, between):
        buffer[0:1, :] = value

        @pl.loop(1, count)
        def _(k):
            pltpu.make_async_remote_copy(
                buffer.at[pl.ds(0, 1)], buffer.at[pl.ds(k, 1)], send, recv,
                device_id=shift(k), device_id_type=MESH,
            ).start()

        between()
        others = buffer.at[pl.ds(1, count - 1)]
        pltpu.make_async_copy(others, others, recv).wait()
        return jnp.sum(buffer[...], axis=0, keepdims=True)

    def all_sent(buffer, send, count):
        others = buffer.at[pl.ds(1, count - 1)]
        pltpu.make_async_copy(others, others, send).wait()

    def tidy_halo():
        copies[2][1](HALF_NEAR)
        for n in range(2):
            for h in range(2):
                moved(own.at[n + 1, pl.ds(h * CELL, CELL)], back_send.at[n, h], homeward(h))

    def tidy_back():
        for n in range(2):
            for b in range(2):
                landed(back.at[n, b], back_recv.at[n, b])
        all_sent(sums_xy, xy_send, nx * ny)

    total = all_sum(
        sums_xy, xy_send, xy_recv, nx * ny,
        lambda k: shifted(lax.div(k, ny), lax.rem(k, ny), 0), row[0:1], tidy_halo,
    )
    total = all_sum(sums_z, z_send, z_recv, nz, lambda k: shifted(0, 0, k), total, tidy_back)
    total = jnp.broadcast_to(total, (SAMPLES, BEAD))
    moments = [total] + [pltpu.roll(total, BEAD - 8 * m, 1) for m in range(1, 6)]
    mix = combination(moments)
    for m in range(3):
        row_buf[m : m + 1, :] = mix[m][0:1]
    row_buf[3:8, :] = jnp.zeros((5, BEAD), f32)
    mixed = jnp.transpose(row_buf[...], (1, 0))[0:SAMPLES]

    for b in range(2):
        for c in range(3):
            rows = slice(c * 8, c * 8 + 8)
            out_ref[b, :, c * BEAD : (c + 1) * BEAD] = (
                mixed[:, 0:1] * start_src[b, rows, :]
                + mixed[:, 1:2] * back[0, b, rows, :]
                + mixed[:, 2:3] * back[1, b, rows, :]
            )

    all_sent(sums_z, z_send, nz)


def body(positions, block_fill, noise, pair_list, pair_count):
    nx, ny, nz = lax.axis_size("gx") // 2, lax.axis_size("gy"), 2 * lax.axis_size("gz")
    dma = pltpu.SemaphoreType.DMA
    vmem, hbm = pl.BlockSpec(memory_space=pltpu.VMEM), pl.BlockSpec(memory_space=pltpu.HBM)
    slots = pair_list.shape[-1]
    out = pl.pallas_call(
        kernel,
        out_shape=jax.ShapeDtypeStruct((2, SAMPLES, 3 * BEAD), f32),
        in_specs=[hbm] * 5,
        out_specs=vmem,
        scratch_shapes=[
            pltpu.VMEM((1, 2), jnp.int32),
            pltpu.VMEM((1, 1), jnp.int32),
            pltpu.VMEM((3, 1, slots), jnp.int32),
            pltpu.VMEM((3, 2, BEAD), f32),
            pltpu.VMEM((2, SAMPLES, WIDTH), f32),
            pltpu.VMEM((2, 8, BEAD), f32),
            pltpu.VMEM((2, CELL, BEAD), f32),
            pltpu.VMEM((9, 4, 8, BEAD), f32),
            pltpu.VMEM((2, CELL, BEAD), f32),
            pltpu.VMEM((3, 9, 112, BEAD), bf16),
            pltpu.VMEM((3, 2 * CELL, BEAD), f32),
            pltpu.VMEM((2, 2, CELL, BEAD), f32),
            pltpu.VMEM((9, 6, 6, BEAD, BEAD), bf16),
            pltpu.VMEM((4, BEAD, 8), f32),
            pltpu.VMEM((2, BEAD, BEAD), f32),
            pltpu.VMEM((nz, BEAD), f32),
            pltpu.VMEM((nx * ny, BEAD), f32),
            pltpu.VMEM((8, BEAD), f32),
            dma((5,)), dma((2, 2)), dma((2, 2)), dma((2, 2)), dma((2, 2)),
            dma((2,)), dma((9,)), dma((3, 2)), dma((3, 9)), dma, dma, dma, dma,
        ],
        compiler_params=pltpu.CompilerParams(
            collective_id=0, has_side_effects=True, vmem_limit_bytes=60 * 1024 * 1024
        ),
    )(
        block_fill.reshape(1, 2), pair_count.reshape(1, 1), pair_list.reshape(3, 1, slots),
        positions.reshape(2, 3, BEAD).transpose(1, 0, 2), noise.reshape(2, SAMPLES, 3 * BEAD),
    )
    return out.reshape(noise.shape)


def solution(mesh):
    cells = P("gx", "gy", "gz", None, None)
    in_specs = (cells, P("gx", "gy", "gz"), cells, cells, P("gx", "gy", "gz"))
    return jax.shard_map(body, mesh=mesh, in_specs=in_specs, out_specs=cells, check_vma=False)
```

```python
import jax
import jax.numpy as jnp
from jax import lax
from jax.experimental import pallas as pl
from jax.experimental.pallas import tpu as pltpu
from jax.sharding import PartitionSpec as P

ROOT_ITERS = 12
RADIUS = 0.08
EPSILON = 1e-6
MESH = pl.DeviceIdType.MESH
BEAD = 128
SAMPLES = 8
CELL = 3 * SAMPLES
LEFT, MID, RIGHT = (0, 32), (32, 48), (80, 32)
PAIRS = ((0, 0), (0, 1), (0, 2), (1, 1), (1, 2), (1, 3))
WIDTH = 3 * BEAD
BLOCKS = ((0, 0), (0, 1), (0, 2), (1, 1), (1, 2), (2, 2))
REACH = 5
NEAR_FIRST = (3, 5, 1, 7, 0, 2, 6, 8)
HALF_NEAR = (5, 7, 6, 8)
f32, bf16 = jnp.float32, jnp.bfloat16


def packed(order):
    return sum(dc * 9**t for t, dc in enumerate(order))


def each_column(order, body, carry=0):
    def step(_, state):
        digits, inside = state
        return lax.div(digits, 9), body(lax.rem(digits, 9), inside)

    return lax.fori_loop(0, len(order), step, (jnp.int32(packed(order)), carry))[1]


def tile_factors(d0, d1, d2):
    dist = d0 * d0 + d1 * d1 + d2 * d2
    root = lax.rsqrt(jnp.maximum(dist, 1e-30))
    capped = jnp.minimum(root, 100.0)
    inv = capped * capped
    length = dist * root
    far_iso = capped * (0.75 * RADIUS + (0.5 * RADIUS**3) * inv)
    far_dyad = capped * (0.75 * RADIUS - (1.5 * RADIUS**3) * inv)
    near_iso = 1.0 - (9.0 / 32.0 / RADIUS) * length
    near_dyad = (3.0 / 32.0 / RADIUS) * length
    apart = dist >= 4.0 * RADIUS * RADIUS
    return jnp.where(apart, far_iso, near_iso), jnp.where(apart, far_dyad, near_dyad) * inv


def inverse_three(m):
    def cof(i, j):
        a, b, c, d = (i + 1) % 3, (i + 2) % 3, (j + 1) % 3, (j + 2) % 3
        return m[a][c] * m[b][d] - m[a][d] * m[b][c]

    co = [[cof(i, j) for j in range(3)] for i in range(3)]
    scale = 1.0 / (m[0][0] * co[0][0] + m[0][1] * co[0][1] + m[0][2] * co[0][2])
    return [[co[j][i] * scale for j in range(3)] for i in range(3)]


def combination(moments):
    def inner(left, right):
        total = 0.0
        for i, a in enumerate(left):
            for j, b in enumerate(right):
                total = total + a * b * moments[i + j]
        return total

    def apply(v):
        return [v[0]] + [v[i] + v[i - 1] for i in range(1, len(v))] + [v[-1]]

    norm = jnp.sqrt(moments[0] + EPSILON)
    v1 = [1.0 / norm]
    w1 = apply(v1)
    a1 = inner(v1, w1)
    r1 = [w1[0] - a1 * v1[0], w1[1]]
    b1 = jnp.sqrt(inner(r1, r1) + EPSILON)
    v2 = [r / b1 for r in r1]
    w2 = apply(v2)
    a2 = inner(v2, w2)
    r2 = [w2[0] - a2 * v2[0] - b1 * v1[0], w2[1] - a2 * v2[1], w2[2]]
    b2 = jnp.sqrt(inner(r2, r2) + EPSILON)
    v3 = [r / b2 for r in r2]
    a3 = inner(v3, apply(v3))
    scale = (a1 + a2 + a3) / 3.0
    zero, one = jnp.zeros_like(a1), jnp.ones_like(a1)
    y = [[e / scale for e in row] for row in ((a1, b1, zero), (b1, a2, b2), (zero, b2, a3))]
    z = [[one if i == j else zero for j in range(3)] for i in range(3)]

    def step(_, state):
        y, z = state
        iz, iy = inverse_three(z), inverse_three(y)
        return (
            [[0.5 * (y[i][j] + iz[i][j]) for j in range(3)] for i in range(3)],
            [[0.5 * (z[i][j] + iy[i][j]) for j in range(3)] for i in range(3)],
        )

    y, z = lax.fori_loop(0, ROOT_ITERS, step, (y, z))
    root = [jnp.sqrt(scale) * y[i][0] for i in range(3)]
    return [
        norm * (root[0] * v1[0] + root[1] * v2[0] + root[2] * v3[0]),
        norm * (root[1] * v2[1] + root[2] * v3[1]),
        norm * (root[2] * v3[2]),
    ]


def kernel(
    fill_hbm, count_hbm, list_hbm, pos_hbm, noise_hbm, out_ref,
    fill_ref, count_ref, list_ref, pos_ref, noise_ref, meta_src, start_src, pos_halo, start_own, halo, own, back, tiles, columns, weights,
    sums_z, sums_xy, row_buf,
    input_sem, move_send, move_recv, back_send, back_recv, pos_send, pos_recv, u_send, u_recv,
    z_send, z_recv, xy_send, xy_recv,
):
    ix, iy, iz = lax.axis_index("gx"), lax.axis_index("gy"), lax.axis_index("gz")
    nx = lax.axis_size("gx") // 2
    ny = lax.axis_size("gy")
    half = lax.axis_size("gz")
    nz = 2 * half
    turn = nz // 4
    my_x, my_z = lax.div(ix, 2), lax.rem(lax.rem(ix, 2) * half + iz + turn, nz)

    def device(x, y, z):
        place = lax.rem(z + nz - turn, nz)
        return (2 * x + lax.div(place, half), y, lax.rem(place, half))

    def shifted(dx, dy, dz):
        return device(
            lax.rem(my_x + dx + nx, nx), lax.rem(iy + dy + ny, ny), lax.rem(my_z + dz + nz, nz)
        )

    inputs = [
        pltpu.make_async_copy(src, dst, input_sem.at[k])
        for k, (src, dst) in enumerate(
            (
                (fill_hbm, fill_ref), (count_hbm, count_ref), (list_hbm, list_ref),
                (pos_hbm, pos_ref), (noise_hbm, noise_ref),
            )
        )
    ]
    for copy in inputs:
        copy.start()

    barrier = pltpu.get_barrier_semaphore()

    def greet(target):
        pl.semaphore_signal(barrier, inc=1, device_id=target, device_id_type=MESH)

    def is_me(target):
        return (target[0] == ix) & (target[2] == iz)

    def greet_other(target):
        @pl.when(jnp.logical_not(is_me(target)))
        def _():
            greet(target)

    for h in range(2):
        greet_other((2 * my_x + h, iy, lax.div(my_z, 2)))
    for k in range(2, REACH + 1):
        greet(shifted(0, 0, k))
        greet(shifted(0, 0, -k))

    @pl.loop(0, 26)
    def _(k):
        q = k + lax.div(k + 13, 26)
        greet(shifted(lax.rem(lax.div(q, 3), 3) - 1, lax.rem(q, 3) - 1, lax.div(q, 9) - 1))

    lanes = lax.broadcasted_iota(jnp.int32, (1, BEAD), 1)
    slots = list_ref.shape[2]
    for copy in inputs:
        copy.wait()
    codes = lax.broadcasted_iota(jnp.int32, (BEAD, slots), 0)
    live = lax.broadcasted_iota(jnp.int32, (1, slots), 1) < count_ref[0:1, 0:1]
    chosen = jnp.where(codes == list_ref[1], 1.0, 0.0).astype(bf16)
    masks = []
    for b in range(2):
        mask = jnp.where(lanes < fill_ref[0:1, b : b + 1], 1.0, 0.0)
        masks.append(mask)
        here = jnp.where(live & (list_ref[0] == b), 1.0, 0.0)
        here = jnp.broadcast_to(here, (SAMPLES, slots)).astype(bf16)
        tally = lax.dot_general(
            here, chosen, (((1,), (1,)), ((), ())), preferred_element_type=f32
        )
        for c in range(3):
            meta_src[b, c : c + 1, :] = pos_ref[c, b : b + 1, :]
        meta_src[b, 3:4, :] = mask
        meta_src[b, 4:5, :] = tally[0:1]
        meta_src[b, 5:8, :] = jnp.zeros((3, BEAD), f32)
        for c in range(3):
            start_src[b, c * 8 : c * 8 + 8, :] = noise_ref[b, :, c * BEAD : (c + 1) * BEAD] * mask

    homes = [device(my_x, iy, 2 * iz + b) for b in range(2)]
    stay = sum(jnp.where(is_me(target), 1, 0) for target in homes)
    pl.semaphore_wait(barrier, 26 + 2 * (REACH - 1) + 2 - stay)

    def move(src, dst, send, recv, target):
        tx, ty, tz = target
        same = (tx == ix) & (tz == iz)

        @pl.when(same)
        def _():
            pltpu.make_async_copy(src, dst, recv).start()

        @pl.when(jnp.logical_not(same))
        def _():
            pltpu.make_async_remote_copy(
                src, dst, send, recv, device_id=target, device_id_type=MESH
            ).start()

    def moved(src, send, target):
        tx, ty, tz = target
        same = (tx == ix) & (tz == iz)

        @pl.when(jnp.logical_not(same))
        def _():
            pltpu.make_async_remote_copy(
                src, src, send, send, device_id=target, device_id_type=MESH
            ).wait_send()

    def landed(dst, recv):
        pltpu.make_async_copy(dst, dst, recv).wait()

    side = lax.rem(ix, 2)
    for b in range(2):
        target = device(my_x, iy, 2 * iz + b)
        move(meta_src.at[b], pos_halo.at[4, 1 + side], move_send.at[0, b], move_recv.at[0, side], target)
    for b in range(2):
        target = device(my_x, iy, 2 * iz + b)
        move(start_src.at[b], start_own.at[side], move_send.at[1, b], move_recv.at[1, side], target)
    for h in range(2):
        landed(pos_halo.at[4, 1 + h], move_recv.at[0, h])

    def exchange(src_of, dst_of, column_of, send, recv):
        def copy(dc, part, dx):
            side_sem = 1 if isinstance(dc, int) else 0
            dy, dz = 1 - lax.rem(dc, 3), 1 - lax.div(dc, 3)
            return pltpu.make_async_remote_copy(
                src_of(part), dst_of(dc, part), send.at[side_sem], recv.at[dc],
                device_id=shifted(dx, dy, dz), device_id_type=MESH,
            )

        def start(order):
            def step(dc, carry):
                copy(dc, 0, 1).start()
                copy(dc, 2, -1).start()
                copy(dc, 1, 0).start()
                return carry

            each_column(order, step)
            copy(4, 0, 1).start()
            copy(4, 2, -1).start()

        def sent(order):
            bytes_of = column_of(slice(0, len(order)))
            pltpu.make_async_copy(bytes_of, bytes_of, send.at[0]).wait()
            sides = dst_of(4, 3)
            pltpu.make_async_copy(sides, sides, send.at[1]).wait()

        def arrived(dc):
            if isinstance(dc, int) and dc == 4:
                sides = dst_of(4, 3)
                pltpu.make_async_copy(sides, sides, recv.at[4]).wait()
            else:
                whole = column_of(dc)
                pltpu.make_async_copy(whole, whole, recv.at[dc]).wait()

        return start, sent, arrived

    def columns_of(ref, dc):
        return ref.at[pl.ds(0, dc.stop)] if isinstance(dc, slice) else ref.at[dc]

    pos_src = {0: (2, 1), 1: (1, 2), 2: (1, 1)}
    pos_dst = {0: (0, 1), 1: (1, 2), 2: (3, 1), 3: (0, 2)}
    pos_start, pos_sent, pos_arrived = exchange(
        lambda part: pos_halo.at[4, pl.ds(*pos_src[part])],
        lambda dc, part: pos_halo.at[dc, pl.ds(*pos_dst[part])],
        lambda dc: columns_of(pos_halo, dc), pos_send, pos_recv,
    )
    pos_start(NEAR_FIRST)

    own_mask = []
    for h in range(2):
        own_mask.append(pos_halo[4, 1 + h, 3:4, :])
        table = jnp.transpose(pos_halo[4, 1 + h], (1, 0))
        weights[h] = jnp.broadcast_to(table[:, 4:5], (BEAD, BEAD))

    u_src = {0: (48, 32), 1: (32, 48), 2: (32, 32)}
    u_dst = {0: LEFT, 1: MID, 2: RIGHT, 3: (0, 64)}

    def u_copy(n):
        return exchange(
            lambda part: halo.at[n, 4, pl.ds(*u_src[part])],
            lambda dc, part: halo.at[n, dc, pl.ds(*u_dst[part])],
            lambda dc: columns_of(halo.at[n], dc), u_send.at[n], u_recv.at[n],
        )

    copies = [u_copy(n) for n in range(3)]
    for h in range(2):
        landed(start_own.at[h], move_recv.at[1, h])
    start = jnp.concatenate([start_own[0], start_own[1]], axis=0)
    own[0] = start
    halo[0, 4, MID[0] : MID[0] + MID[1], :] = start.astype(bf16)
    copies[0][0](NEAR_FIRST)

    def build(dc, pairs=(0, 1, 2, 3, 4, 5)):
        for xs in sorted({PAIRS[q][1] for q in pairs}):
            columns[xs] = jnp.transpose(pos_halo[dc, xs], (1, 0))
        mine = [[pos_halo[4, 1 + a, c : c + 1, :] for c in range(3)] for a in range(2)]

        @pl.loop(0, BEAD // 16, unroll=8)
        def _(r):
            row = pl.multiple_of(r * 16, 16)
            away = {}
            for xs in sorted({PAIRS[q][1] for q in pairs}):
                block = columns[xs, pl.ds(row, 16), :]
                away[xs] = [jnp.broadcast_to(block[:, c : c + 1], (16, BEAD)) for c in range(3)]
            for q in pairs:
                a, xs = PAIRS[q]
                d = [away[xs][c] - mine[a][c] for c in range(3)]
                iso, dyad = tile_factors(*d)
                scaled = [dyad * d[c] for c in range(3)]
                for k, (c, e) in enumerate(BLOCKS):
                    entry = scaled[c] * d[e]
                    entry = entry + iso if c == e else entry
                    tiles[dc, q, k, pl.ds(row, 16), :] = entry.astype(bf16)

    def products(n, a, dc, first, count):
        entries, blocks = [], []
        u = halo[n, dc].astype(f32)
        row, deep = (dc % 3, dc // 3) if isinstance(dc, int) else (lax.rem(dc, 3), lax.div(dc, 3))
        for xs in range(a + first, a + first + count):
            weight = weights[a, pl.ds(9 * (xs - a) + 3 * row + deep, 1), :]
            for e in range(3):
                entries.append(u[8 + 24 * xs + 8 * e : 16 + 24 * xs + 8 * e] * weight)
                parts = [
                    tiles[dc, 2 * a + xs, BLOCKS.index((min(c, e), max(c, e)))] for c in range(3)
                ]
                blocks.append(jnp.concatenate(parts, axis=1))
        total = None
        for x in range(count):
            left = jnp.concatenate(entries[3 * x : 3 * x + 3], axis=1).astype(bf16)
            right = jnp.concatenate(blocks[3 * x : 3 * x + 3], axis=0)
            term = jnp.dot(left, right, preferred_element_type=f32)
            total = term if total is None else total + term
        return total

    build(4, (1, 2, 3, 4))
    pos_arrived(4)
    build(4, (0, 5))
    copies[0][2](4)

    def build_next(dc, state):
        before, left, right = state
        pos_arrived(dc)
        left = left + products(0, 0, before, 0, 3)
        right = right + products(0, 1, before, 0, 3)
        build(dc)
        copies[0][2](dc)
        return dc, left, right

    blank = jnp.zeros((SAMPLES, WIDTH), f32)
    state = each_column(NEAR_FIRST, build_next, (jnp.int32(4), blank, blank))
    image = [state[1 + a] + products(0, a, state[0], 0, 3) for a in range(2)]

    def matvec(n):
        arrived = copies[n][2]
        if n == 0:
            acc = image
        elif n == 1:
            acc = [0.0, 0.0]
            for dc in (4, *NEAR_FIRST):
                arrived(dc)
                acc = [acc[a] + products(n, a, dc, 0, 3) for a in range(2)]
        else:
            arrived(4)
            acc = [products(n, a, 4, 2, 1) for a in range(2)]
            for dc in HALF_NEAR:
                arrived(dc)
                acc = [acc[a] + products(n, a, dc, 0, 3) for a in range(2)]
            acc = [2.0 * acc[a] + products(n, a, 4, 1, 1) for a in range(2)]
        rows = []
        for a in range(2):
            for c in range(3):
                rows.append(acc[a][:, c * BEAD : (c + 1) * BEAD] * own_mask[a])
        full = jnp.concatenate(rows, axis=0)
        return full - halo[n, 4, MID[0] : MID[0] + MID[1], :].astype(f32)

    def fold(left, right):
        product = left * right
        total = product[0:8]
        for k in range(1, 6):
            total = total + product[8 * k : 8 * k + 8]
        return total

    def homeward(h):
        return (2 * my_x + h, iy, lax.div(my_z, 2))

    current = own[0]
    parts = [fold(current, current)]
    for n in range(2):
        nxt = matvec(n)
        own[n + 1] = nxt
        halo[n + 1, 4, MID[0] : MID[0] + MID[1], :] = nxt.astype(bf16)
        copies[n + 1][0](NEAR_FIRST if n == 0 else HALF_NEAR)
        for h in range(2):
            move(
                own.at[n + 1, pl.ds(h * CELL, CELL)], back.at[n, lax.rem(my_z, 2)],
                back_send.at[n, h], back_recv.at[n, lax.rem(my_z, 2)], homeward(h),
            )
        parts += [fold(current, nxt), fold(nxt, nxt)]
        current = nxt
        copies[n][1](NEAR_FIRST)
        if n == 0:
            pos_sent(NEAR_FIRST)
            for b in range(2):
                target = device(my_x, iy, 2 * iz + b)
                moved(meta_src.at[b], move_send.at[0, b], target)
                moved(start_src.at[b], move_send.at[1, b], target)
    parts.append(fold(current, matvec(2)))

    ones = jnp.ones((SAMPLES, BEAD), f32)
    row = lax.dot_general(
        ones, jnp.concatenate(parts + [jnp.zeros((BEAD - 48, BEAD), f32)], axis=0),
        (((1,), (1,)), ((), ())), precision=lax.Precision.HIGHEST, preferred_element_type=f32,
    )

    def all_sum(buffer, send, recv, count, shift, value, between):
        buffer[0:1, :] = value

        @pl.loop(1, count)
        def _(k):
            pltpu.make_async_remote_copy(
                buffer.at[pl.ds(0, 1)], buffer.at[pl.ds(k, 1)], send, recv,
                device_id=shift(k), device_id_type=MESH,
            ).start()

        between()
        others = buffer.at[pl.ds(1, count - 1)]
        pltpu.make_async_copy(others, others, recv).wait()
        return jnp.sum(buffer[...], axis=0, keepdims=True)

    def all_sent(buffer, send, count):
        others = buffer.at[pl.ds(1, count - 1)]
        pltpu.make_async_copy(others, others, send).wait()

    def tidy_halo():
        copies[2][1](HALF_NEAR)
        for n in range(2):
            for h in range(2):
                moved(own.at[n + 1, pl.ds(h * CELL, CELL)], back_send.at[n, h], homeward(h))

    def tidy_back():
        for n in range(2):
            for b in range(2):
                landed(back.at[n, b], back_recv.at[n, b])
        all_sent(sums_xy, xy_send, nx * ny)

    total = all_sum(
        sums_xy, xy_send, xy_recv, nx * ny,
        lambda k: shifted(lax.div(k, ny), lax.rem(k, ny), 0), row[0:1], tidy_halo,
    )
    total = all_sum(sums_z, z_send, z_recv, nz, lambda k: shifted(0, 0, k), total, tidy_back)
    total = jnp.broadcast_to(total, (SAMPLES, BEAD))
    moments = [total] + [pltpu.roll(total, BEAD - 8 * m, 1) for m in range(1, 6)]
    mix = combination(moments)
    for m in range(3):
        row_buf[m : m + 1, :] = mix[m][0:1]
    row_buf[3:8, :] = jnp.zeros((5, BEAD), f32)
    mixed = jnp.transpose(row_buf[...], (1, 0))[0:SAMPLES]

    for b in range(2):
        for c in range(3):
            rows = slice(c * 8, c * 8 + 8)
            out_ref[b, :, c * BEAD : (c + 1) * BEAD] = (
                mixed[:, 0:1] * start_src[b, rows, :]
                + mixed[:, 1:2] * back[0, b, rows, :]
                + mixed[:, 2:3] * back[1, b, rows, :]
            )

    all_sent(sums_z, z_send, nz)


def body(positions, block_fill, noise, pair_list, pair_count):
    nx, ny, nz = lax.axis_size("gx") // 2, lax.axis_size("gy"), 2 * lax.axis_size("gz")
    dma = pltpu.SemaphoreType.DMA
    vmem, hbm = pl.BlockSpec(memory_space=pltpu.VMEM), pl.BlockSpec(memory_space=pltpu.HBM)
    slots = pair_list.shape[-1]
    out = pl.pallas_call(
        kernel,
        out_shape=jax.ShapeDtypeStruct((2, SAMPLES, 3 * BEAD), f32),
        in_specs=[hbm] * 5,
        out_specs=vmem,
        scratch_shapes=[
            pltpu.VMEM((1, 2), jnp.int32),
            pltpu.VMEM((1, 1), jnp.int32),
            pltpu.VMEM((3, 1, slots), jnp.int32),
            pltpu.VMEM((3, 2, BEAD), f32),
            pltpu.VMEM((2, SAMPLES, WIDTH), f32),
            pltpu.VMEM((2, 8, BEAD), f32),
            pltpu.VMEM((2, CELL, BEAD), f32),
            pltpu.VMEM((9, 4, 8, BEAD), f32),
            pltpu.VMEM((2, CELL, BEAD), f32),
            pltpu.VMEM((3, 9, 112, BEAD), bf16),
            pltpu.VMEM((3, 2 * CELL, BEAD), f32),
            pltpu.VMEM((2, 2, CELL, BEAD), f32),
            pltpu.VMEM((9, 6, 6, BEAD, BEAD), bf16),
            pltpu.VMEM((4, BEAD, 8), f32),
            pltpu.VMEM((2, BEAD, BEAD), f32),
            pltpu.VMEM((nz, BEAD), f32),
            pltpu.VMEM((nx * ny, BEAD), f32),
            pltpu.VMEM((8, BEAD), f32),
            dma((5,)), dma((2, 2)), dma((2, 2)), dma((2, 2)), dma((2, 2)),
            dma((2,)), dma((9,)), dma((3, 2)), dma((3, 9)), dma, dma, dma, dma,
        ],
        compiler_params=pltpu.CompilerParams(
            collective_id=0, has_side_effects=True, vmem_limit_bytes=60 * 1024 * 1024
        ),
    )(
        block_fill.reshape(1, 2), pair_count.reshape(1, 1), pair_list.reshape(3, 1, slots),
        positions.reshape(2, 3, BEAD).transpose(1, 0, 2), noise.reshape(2, SAMPLES, 3 * BEAD),
    )
    return out.reshape(noise.shape)


def solution(mesh):
    cells = P("gx", "gy", "gz", None, None)
    in_specs = (cells, P("gx", "gy", "gz"), cells, cells, P("gx", "gy", "gz"))
    return jax.shard_map(body, mesh=mesh, in_specs=in_specs, out_specs=cells, check_vma=False)
```

```python
import jax
import jax.numpy as jnp
from jax import lax
from jax.experimental import pallas as pl
from jax.experimental.pallas import tpu as pltpu
from jax.sharding import PartitionSpec as P

ROOT_ITERS = 12
RADIUS = 0.08
EPSILON = 1e-6
MESH = pl.DeviceIdType.MESH
BEAD = 128
SAMPLES = 8
CELL = 3 * SAMPLES
LEFT, MID, RIGHT = (0, 32), (32, 48), (80, 32)
PAIRS = ((0, 0), (0, 1), (0, 2), (1, 1), (1, 2), (1, 3))
WIDTH = 3 * BEAD
BLOCKS = ((0, 0), (0, 1), (0, 2), (1, 1), (1, 2), (2, 2))
REACH = 5
NEAR_FIRST = (3, 5, 1, 7, 0, 2, 6, 8)
HALF_NEAR = (5, 7, 6, 8)
f32, bf16 = jnp.float32, jnp.bfloat16


def packed(order):
    return sum(dc * 9**t for t, dc in enumerate(order))


def each_column(order, body, carry=0):
    def step(_, state):
        digits, inside = state
        return lax.div(digits, 9), body(lax.rem(digits, 9), inside)

    return lax.fori_loop(0, len(order), step, (jnp.int32(packed(order)), carry))[1]


def tile_factors(d0, d1, d2):
    dist = d0 * d0 + d1 * d1 + d2 * d2
    root = lax.rsqrt(jnp.maximum(dist, 1e-30))
    capped = jnp.minimum(root, 100.0)
    inv = capped * capped
    length = dist * root
    far_iso = capped * (0.75 * RADIUS + (0.5 * RADIUS**3) * inv)
    far_dyad = capped * (0.75 * RADIUS - (1.5 * RADIUS**3) * inv)
    near_iso = 1.0 - (9.0 / 32.0 / RADIUS) * length
    near_dyad = (3.0 / 32.0 / RADIUS) * length
    apart = dist >= 4.0 * RADIUS * RADIUS
    return jnp.where(apart, far_iso, near_iso), jnp.where(apart, far_dyad, near_dyad) * inv


def inverse_three(m):
    def cof(i, j):
        a, b, c, d = (i + 1) % 3, (i + 2) % 3, (j + 1) % 3, (j + 2) % 3
        return m[a][c] * m[b][d] - m[a][d] * m[b][c]

    co = [[cof(i, j) for j in range(3)] for i in range(3)]
    scale = 1.0 / (m[0][0] * co[0][0] + m[0][1] * co[0][1] + m[0][2] * co[0][2])
    return [[co[j][i] * scale for j in range(3)] for i in range(3)]


def combination(moments):
    def inner(left, right):
        total = 0.0
        for i, a in enumerate(left):
            for j, b in enumerate(right):
                total = total + a * b * moments[i + j]
        return total

    def apply(v):
        return [v[0]] + [v[i] + v[i - 1] for i in range(1, len(v))] + [v[-1]]

    norm = jnp.sqrt(moments[0] + EPSILON)
    v1 = [1.0 / norm]
    w1 = apply(v1)
    a1 = inner(v1, w1)
    r1 = [w1[0] - a1 * v1[0], w1[1]]
    b1 = jnp.sqrt(inner(r1, r1) + EPSILON)
    v2 = [r / b1 for r in r1]
    w2 = apply(v2)
    a2 = inner(v2, w2)
    r2 = [w2[0] - a2 * v2[0] - b1 * v1[0], w2[1] - a2 * v2[1], w2[2]]
    b2 = jnp.sqrt(inner(r2, r2) + EPSILON)
    v3 = [r / b2 for r in r2]
    a3 = inner(v3, apply(v3))
    scale = (a1 + a2 + a3) / 3.0
    zero, one = jnp.zeros_like(a1), jnp.ones_like(a1)
    y = [[e / scale for e in row] for row in ((a1, b1, zero), (b1, a2, b2), (zero, b2, a3))]
    z = [[one if i == j else zero for j in range(3)] for i in range(3)]

    def step(_, state):
        y, z = state
        iz, iy = inverse_three(z), inverse_three(y)
        return (
            [[0.5 * (y[i][j] + iz[i][j]) for j in range(3)] for i in range(3)],
            [[0.5 * (z[i][j] + iy[i][j]) for j in range(3)] for i in range(3)],
        )

    y, z = lax.fori_loop(0, ROOT_ITERS, step, (y, z))
    root = [jnp.sqrt(scale) * y[i][0] for i in range(3)]
    return [
        norm * (root[0] * v1[0] + root[1] * v2[0] + root[2] * v3[0]),
        norm * (root[1] * v2[1] + root[2] * v3[1]),
        norm * (root[2] * v3[2]),
    ]


def kernel(
    fill_hbm, count_hbm, list_hbm, pos_hbm, noise_hbm, out_ref,
    fill_ref, count_ref, list_ref, pos_ref, noise_ref, meta_src, start_src, pos_halo, start_own, halo, own, back, tiles, columns, weights,
    sums_z, sums_xy, row_buf,
    input_sem, move_send, move_recv, back_send, back_recv, pos_send, pos_recv, u_send, u_recv,
    z_send, z_recv, xy_send, xy_recv,
):
    ix, iy, iz = lax.axis_index("gx"), lax.axis_index("gy"), lax.axis_index("gz")
    nx = lax.axis_size("gx") // 2
    ny = lax.axis_size("gy")
    half = lax.axis_size("gz")
    nz = 2 * half
    turn = nz // 4
    my_x, my_z = lax.div(ix, 2), lax.rem(lax.rem(ix, 2) * half + iz + turn, nz)

    def device(x, y, z):
        place = lax.rem(z + nz - turn, nz)
        return (2 * x + lax.div(place, half), y, lax.rem(place, half))

    def shifted(dx, dy, dz):
        return device(
            lax.rem(my_x + dx + nx, nx), lax.rem(iy + dy + ny, ny), lax.rem(my_z + dz + nz, nz)
        )

    inputs = [
        pltpu.make_async_copy(src, dst, input_sem.at[k])
        for k, (src, dst) in enumerate(
            (
                (fill_hbm, fill_ref), (count_hbm, count_ref), (list_hbm, list_ref),
                (pos_hbm, pos_ref), (noise_hbm, noise_ref),
            )
        )
    ]
    for copy in inputs:
        copy.start()

    barrier = pltpu.get_barrier_semaphore()

    def greet(target):
        pl.semaphore_signal(barrier, inc=1, device_id=target, device_id_type=MESH)

    def is_me(target):
        return (target[0] == ix) & (target[2] == iz)

    def greet_other(target):
        @pl.when(jnp.logical_not(is_me(target)))
        def _():
            greet(target)

    for h in range(2):
        greet_other((2 * my_x + h, iy, lax.div(my_z, 2)))
    for k in range(2, REACH + 1):
        greet(shifted(0, 0, k))
        greet(shifted(0, 0, -k))

    @pl.loop(0, 26)
    def _(k):
        q = k + lax.div(k + 13, 26)
        greet(shifted(lax.rem(lax.div(q, 3), 3) - 1, lax.rem(q, 3) - 1, lax.div(q, 9) - 1))

    lanes = lax.broadcasted_iota(jnp.int32, (1, BEAD), 1)
    slots = list_ref.shape[2]
    for copy in inputs:
        copy.wait()
    codes = lax.broadcasted_iota(jnp.int32, (BEAD, slots), 0)
    live = lax.broadcasted_iota(jnp.int32, (1, slots), 1) < count_ref[0:1, 0:1]
    chosen = jnp.where(codes == list_ref[1], 1.0, 0.0).astype(bf16)
    masks = []
    for b in range(2):
        mask = jnp.where(lanes < fill_ref[0:1, b : b + 1], 1.0, 0.0)
        masks.append(mask)
        here = jnp.where(live & (list_ref[0] == b), 1.0, 0.0)
        here = jnp.broadcast_to(here, (SAMPLES, slots)).astype(bf16)
        tally = lax.dot_general(
            here, chosen, (((1,), (1,)), ((), ())), preferred_element_type=f32
        )
        for c in range(3):
            meta_src[b, c : c + 1, :] = pos_ref[c, b : b + 1, :]
        meta_src[b, 3:4, :] = mask
        meta_src[b, 4:5, :] = tally[0:1]
        meta_src[b, 5:8, :] = jnp.zeros((3, BEAD), f32)
        for c in range(3):
            start_src[b, c * 8 : c * 8 + 8, :] = noise_ref[b, :, c * BEAD : (c + 1) * BEAD] * mask

    homes = [device(my_x, iy, 2 * iz + b) for b in range(2)]
    stay = sum(jnp.where(is_me(target), 1, 0) for target in homes)
    pl.semaphore_wait(barrier, 26 + 2 * (REACH - 1) + 2 - stay)

    def move(src, dst, send, recv, target):
        tx, ty, tz = target
        same = (tx == ix) & (tz == iz)

        @pl.when(same)
        def _():
            pltpu.make_async_copy(src, dst, recv).start()

        @pl.when(jnp.logical_not(same))
        def _():
            pltpu.make_async_remote_copy(
                src, dst, send, recv, device_id=target, device_id_type=MESH
            ).start()

    def moved(src, send, target):
        tx, ty, tz = target
        same = (tx == ix) & (tz == iz)

        @pl.when(jnp.logical_not(same))
        def _():
            pltpu.make_async_remote_copy(
                src, src, send, send, device_id=target, device_id_type=MESH
            ).wait_send()

    def landed(dst, recv):
        pltpu.make_async_copy(dst, dst, recv).wait()

    side = lax.rem(ix, 2)
    for b in range(2):
        target = device(my_x, iy, 2 * iz + b)
        move(meta_src.at[b], pos_halo.at[4, 1 + side], move_send.at[0, b], move_recv.at[0, side], target)
    for b in range(2):
        target = device(my_x, iy, 2 * iz + b)
        move(start_src.at[b], start_own.at[side], move_send.at[1, b], move_recv.at[1, side], target)
    for h in range(2):
        landed(pos_halo.at[4, 1 + h], move_recv.at[0, h])

    def exchange(src_of, dst_of, column_of, send, recv):
        def copy(dc, part, dx):
            side_sem = 1 if isinstance(dc, int) else 0
            dy, dz = 1 - lax.rem(dc, 3), 1 - lax.div(dc, 3)
            return pltpu.make_async_remote_copy(
                src_of(part), dst_of(dc, part), send.at[side_sem], recv.at[dc],
                device_id=shifted(dx, dy, dz), device_id_type=MESH,
            )

        def start(order):
            def step(dc, carry):
                copy(dc, 0, 1).start()
                copy(dc, 2, -1).start()
                copy(dc, 1, 0).start()
                return carry

            each_column(order, step)
            copy(4, 0, 1).start()
            copy(4, 2, -1).start()

        def sent(order):
            bytes_of = column_of(slice(0, len(order)))
            pltpu.make_async_copy(bytes_of, bytes_of, send.at[0]).wait()
            sides = dst_of(4, 3)
            pltpu.make_async_copy(sides, sides, send.at[1]).wait()

        def arrived(dc):
            if isinstance(dc, int) and dc == 4:
                sides = dst_of(4, 3)
                pltpu.make_async_copy(sides, sides, recv.at[4]).wait()
            else:
                whole = column_of(dc)
                pltpu.make_async_copy(whole, whole, recv.at[dc]).wait()

        return start, sent, arrived

    def columns_of(ref, dc):
        return ref.at[pl.ds(0, dc.stop)] if isinstance(dc, slice) else ref.at[dc]

    def pos_rows(dc):
        if isinstance(dc, slice):
            return pos_halo.at[pl.ds(0, dc.stop), pl.ds(0, 4), pl.ds(0, 4)]
        return pos_halo.at[dc, pl.ds(0, 4), pl.ds(0, 4)]

    pos_src = {0: (2, 1), 1: (1, 2), 2: (1, 1)}
    pos_dst = {0: (0, 1), 1: (1, 2), 2: (3, 1), 3: (0, 2)}
    pos_start, pos_sent, pos_arrived = exchange(
        lambda part: pos_halo.at[4, pl.ds(*pos_src[part]), pl.ds(0, 4)],
        lambda dc, part: pos_halo.at[dc, pl.ds(*pos_dst[part]), pl.ds(0, 4)],
        lambda dc: pos_rows(dc), pos_send, pos_recv,
    )
    pos_start(NEAR_FIRST)

    own_mask = []
    for h in range(2):
        own_mask.append(pos_halo[4, 1 + h, 3:4, :])
        table = jnp.transpose(pos_halo[4, 1 + h], (1, 0))
        weights[h] = jnp.broadcast_to(table[:, 4:5], (BEAD, BEAD))

    u_src = {0: (48, 32), 1: (32, 48), 2: (32, 32)}
    u_dst = {0: LEFT, 1: MID, 2: RIGHT, 3: (0, 64)}

    def u_copy(n):
        return exchange(
            lambda part: halo.at[n, 4, pl.ds(*u_src[part])],
            lambda dc, part: halo.at[n, dc, pl.ds(*u_dst[part])],
            lambda dc: columns_of(halo.at[n], dc), u_send.at[n], u_recv.at[n],
        )

    copies = [u_copy(n) for n in range(3)]
    for h in range(2):
        landed(start_own.at[h], move_recv.at[1, h])
    start = jnp.concatenate([start_own[0], start_own[1]], axis=0)
    own[0] = start
    halo[0, 4, MID[0] : MID[0] + MID[1], :] = start.astype(bf16)
    copies[0][0](NEAR_FIRST)

    def build(dc, pairs=(0, 1, 2, 3, 4, 5)):
        for xs in sorted({PAIRS[q][1] for q in pairs}):
            columns[xs] = jnp.transpose(pos_halo[dc, xs], (1, 0))
        mine = [[pos_halo[4, 1 + a, c : c + 1, :] for c in range(3)] for a in range(2)]

        @pl.loop(0, BEAD // 16, unroll=8)
        def _(r):
            row = pl.multiple_of(r * 16, 16)
            away = {}
            for xs in sorted({PAIRS[q][1] for q in pairs}):
                block = columns[xs, pl.ds(row, 16), :]
                away[xs] = [jnp.broadcast_to(block[:, c : c + 1], (16, BEAD)) for c in range(3)]
            for q in pairs:
                a, xs = PAIRS[q]
                d = [away[xs][c] - mine[a][c] for c in range(3)]
                iso, dyad = tile_factors(*d)
                scaled = [dyad * d[c] for c in range(3)]
                for k, (c, e) in enumerate(BLOCKS):
                    entry = scaled[c] * d[e]
                    entry = entry + iso if c == e else entry
                    tiles[dc, q, k, pl.ds(row, 16), :] = entry.astype(bf16)

    def products(n, a, dc, first, count):
        entries, blocks = [], []
        u = halo[n, dc].astype(f32)
        row, deep = (dc % 3, dc // 3) if isinstance(dc, int) else (lax.rem(dc, 3), lax.div(dc, 3))
        for xs in range(a + first, a + first + count):
            weight = weights[a, pl.ds(9 * (xs - a) + 3 * row + deep, 1), :]
            for e in range(3):
                entries.append(u[8 + 24 * xs + 8 * e : 16 + 24 * xs + 8 * e] * weight)
                parts = [
                    tiles[dc, 2 * a + xs, BLOCKS.index((min(c, e), max(c, e)))] for c in range(3)
                ]
                blocks.append(jnp.concatenate(parts, axis=1))
        total = None
        for x in range(count):
            left = jnp.concatenate(entries[3 * x : 3 * x + 3], axis=1).astype(bf16)
            right = jnp.concatenate(blocks[3 * x : 3 * x + 3], axis=0)
            term = jnp.dot(left, right, preferred_element_type=f32)
            total = term if total is None else total + term
        return total

    build(4, (1, 2, 3, 4))
    pos_arrived(4)
    build(4, (0, 5))
    copies[0][2](4)

    def build_next(dc, state):
        before, left, right = state
        pos_arrived(dc)
        left = left + products(0, 0, before, 0, 3)
        right = right + products(0, 1, before, 0, 3)
        build(dc)
        copies[0][2](dc)
        return dc, left, right

    blank = jnp.zeros((SAMPLES, WIDTH), f32)
    state = each_column(NEAR_FIRST, build_next, (jnp.int32(4), blank, blank))
    image = [state[1 + a] + products(0, a, state[0], 0, 3) for a in range(2)]

    def matvec(n):
        arrived = copies[n][2]
        if n == 0:
            acc = image
        elif n == 1:
            acc = [0.0, 0.0]
            for dc in (4, *NEAR_FIRST):
                arrived(dc)
                acc = [acc[a] + products(n, a, dc, 0, 3) for a in range(2)]
        else:
            arrived(4)
            acc = [products(n, a, 4, 2, 1) for a in range(2)]
            for dc in HALF_NEAR:
                arrived(dc)
                acc = [acc[a] + products(n, a, dc, 0, 3) for a in range(2)]
            acc = [2.0 * acc[a] + products(n, a, 4, 1, 1) for a in range(2)]
        rows = []
        for a in range(2):
            for c in range(3):
                rows.append(acc[a][:, c * BEAD : (c + 1) * BEAD] * own_mask[a])
        full = jnp.concatenate(rows, axis=0)
        return full - halo[n, 4, MID[0] : MID[0] + MID[1], :].astype(f32)

    def fold(left, right):
        product = left * right
        total = product[0:8]
        for k in range(1, 6):
            total = total + product[8 * k : 8 * k + 8]
        return total

    def homeward(h):
        return (2 * my_x + h, iy, lax.div(my_z, 2))

    current = own[0]
    parts = [fold(current, current)]
    for n in range(2):
        nxt = matvec(n)
        own[n + 1] = nxt
        halo[n + 1, 4, MID[0] : MID[0] + MID[1], :] = nxt.astype(bf16)
        copies[n + 1][0](NEAR_FIRST if n == 0 else HALF_NEAR)
        for h in range(2):
            move(
                own.at[n + 1, pl.ds(h * CELL, CELL)], back.at[n, lax.rem(my_z, 2)],
                back_send.at[n, h], back_recv.at[n, lax.rem(my_z, 2)], homeward(h),
            )
        parts += [fold(current, nxt), fold(nxt, nxt)]
        current = nxt
        copies[n][1](NEAR_FIRST)
        if n == 0:
            pos_sent(NEAR_FIRST)
            for b in range(2):
                target = device(my_x, iy, 2 * iz + b)
                moved(meta_src.at[b], move_send.at[0, b], target)
                moved(start_src.at[b], move_send.at[1, b], target)
    parts.append(fold(current, matvec(2)))

    ones = jnp.ones((SAMPLES, BEAD), f32)
    row = lax.dot_general(
        ones, jnp.concatenate(parts + [jnp.zeros((BEAD - 48, BEAD), f32)], axis=0),
        (((1,), (1,)), ((), ())), precision=lax.Precision.HIGHEST, preferred_element_type=f32,
    )

    def all_sum(buffer, send, recv, count, shift, value, between):
        buffer[0:1, :] = value

        @pl.loop(1, count)
        def _(k):
            pltpu.make_async_remote_copy(
                buffer.at[pl.ds(0, 1)], buffer.at[pl.ds(k, 1)], send, recv,
                device_id=shift(k), device_id_type=MESH,
            ).start()

        between()
        others = buffer.at[pl.ds(1, count - 1)]
        pltpu.make_async_copy(others, others, recv).wait()
        return jnp.sum(buffer[...], axis=0, keepdims=True)

    def all_sent(buffer, send, count):
        others = buffer.at[pl.ds(1, count - 1)]
        pltpu.make_async_copy(others, others, send).wait()

    def tidy_halo():
        copies[2][1](HALF_NEAR)
        for n in range(2):
            for h in range(2):
                moved(own.at[n + 1, pl.ds(h * CELL, CELL)], back_send.at[n, h], homeward(h))

    def tidy_back():
        for n in range(2):
            for b in range(2):
                landed(back.at[n, b], back_recv.at[n, b])
        all_sent(sums_xy, xy_send, nx * ny)

    total = all_sum(
        sums_xy, xy_send, xy_recv, nx * ny,
        lambda k: shifted(lax.div(k, ny), lax.rem(k, ny), 0), row[0:1], tidy_halo,
    )
    total = all_sum(sums_z, z_send, z_recv, nz, lambda k: shifted(0, 0, k), total, tidy_back)
    total = jnp.broadcast_to(total, (SAMPLES, BEAD))
    moments = [total] + [pltpu.roll(total, BEAD - 8 * m, 1) for m in range(1, 6)]
    mix = combination(moments)
    for m in range(3):
        row_buf[m : m + 1, :] = mix[m][0:1]
    row_buf[3:8, :] = jnp.zeros((5, BEAD), f32)
    mixed = jnp.transpose(row_buf[...], (1, 0))[0:SAMPLES]

    for b in range(2):
        for c in range(3):
            rows = slice(c * 8, c * 8 + 8)
            out_ref[b, :, c * BEAD : (c + 1) * BEAD] = (
                mixed[:, 0:1] * start_src[b, rows, :]
                + mixed[:, 1:2] * back[0, b, rows, :]
                + mixed[:, 2:3] * back[1, b, rows, :]
            )

    all_sent(sums_z, z_send, nz)


def body(positions, block_fill, noise, pair_list, pair_count):
    nx, ny, nz = lax.axis_size("gx") // 2, lax.axis_size("gy"), 2 * lax.axis_size("gz")
    dma = pltpu.SemaphoreType.DMA
    vmem, hbm = pl.BlockSpec(memory_space=pltpu.VMEM), pl.BlockSpec(memory_space=pltpu.HBM)
    slots = pair_list.shape[-1]
    out = pl.pallas_call(
        kernel,
        out_shape=jax.ShapeDtypeStruct((2, SAMPLES, 3 * BEAD), f32),
        in_specs=[hbm] * 5,
        out_specs=vmem,
        scratch_shapes=[
            pltpu.VMEM((1, 2), jnp.int32),
            pltpu.VMEM((1, 1), jnp.int32),
            pltpu.VMEM((3, 1, slots), jnp.int32),
            pltpu.VMEM((3, 2, BEAD), f32),
            pltpu.VMEM((2, SAMPLES, WIDTH), f32),
            pltpu.VMEM((2, 8, BEAD), f32),
            pltpu.VMEM((2, CELL, BEAD), f32),
            pltpu.VMEM((9, 4, 8, BEAD), f32),
            pltpu.VMEM((2, CELL, BEAD), f32),
            pltpu.VMEM((3, 9, 112, BEAD), bf16),
            pltpu.VMEM((3, 2 * CELL, BEAD), f32),
            pltpu.VMEM((2, 2, CELL, BEAD), f32),
            pltpu.VMEM((9, 6, 6, BEAD, BEAD), bf16),
            pltpu.VMEM((4, BEAD, 8), f32),
            pltpu.VMEM((2, BEAD, BEAD), f32),
            pltpu.VMEM((nz, BEAD), f32),
            pltpu.VMEM((nx * ny, BEAD), f32),
            pltpu.VMEM((8, BEAD), f32),
            dma((5,)), dma((2, 2)), dma((2, 2)), dma((2, 2)), dma((2, 2)),
            dma((2,)), dma((9,)), dma((3, 2)), dma((3, 9)), dma, dma, dma, dma,
        ],
        compiler_params=pltpu.CompilerParams(
            collective_id=0, has_side_effects=True, vmem_limit_bytes=60 * 1024 * 1024
        ),
    )(
        block_fill.reshape(1, 2), pair_count.reshape(1, 1), pair_list.reshape(3, 1, slots),
        positions.reshape(2, 3, BEAD).transpose(1, 0, 2), noise.reshape(2, SAMPLES, 3 * BEAD),
    )
    return out.reshape(noise.shape)


def solution(mesh):
    cells = P("gx", "gy", "gz", None, None)
    in_specs = (cells, P("gx", "gy", "gz"), cells, cells, P("gx", "gy", "gz"))
    return jax.shard_map(body, mesh=mesh, in_specs=in_specs, out_specs=cells, check_vma=False)
```
